32 devices in a mesh: rep: 2 (over y), blk: 4 (over z), mpo: 4 (over x, core).
Axes of the slice: x: 2, y: 2, z: 4, core: 2. Of those that a mesh axis runs over, the one named last changes fastest.
Arguments:
- wavefunction: bfloat16 [1024, 4096], P('rep', 'blk'), parts along dimension 0, may hold values from -6 to 6
- left_blocks: bfloat16 [32, 4, 128, 128], P(('rep', 'mpo'), 'blk'), parts along dimension 0, may hold values from -0.125 to 0.125
- right_blocks: bfloat16 [32, 2, 128, 128], P(('rep', 'mpo')), parts along dimension 0, may hold values from -0.5 to 0.5
- site_terms: bfloat16 [32, 16, 16], P(('rep', 'mpo')), parts along dimension 0, may hold values from -1.5 to 1.5
- left_source: int32 [32, 4], P(('rep', 'mpo')), parts along dimension 0, may hold values from 0 to 3
- right_source: int32 [32, 2], P(('rep', 'mpo')), parts along dimension 0, may hold values from 0 to 1
- live_pairs: int32 [8, 2], P('rep'), parts along dimension 0, may hold values 0 or 1
Outputs:
- sigma_vector: bfloat16 [1024, 4096], P(('rep', 'blk'), 'mpo'), parts along dimension 0
The draws below stay inside these ranges and needn't reach their ends.
There are 2 independent parts, one for each index of `rep`. The reference program is written for one: setup_inputs(seed, part) draws one part's arguments, and reference() takes and returns one part's arrays. A program takes and returns all parts, laid end to end along the dimension named above; each array names one. Nothing has to cross between parts.
Inputs may be any that keep to these rules, and one draw needn't show every extreme that they name: left_source[w, a] is the left block of the wavefunction that term w carries into left block a. right_source[w, b] is the right block that term w carries into right block b. `live_pairs`: 1 where the pair of blocks is allowed by the quantum numbers.
All inputs are finite; a program needn't handle non-finite values.
Results may differ from the reference program's by a relative error of at most 0.0057.
Values may be sent and summed in bfloat16 or wider, within the bound.
No kernel may reach another device: no remote copies, remote signals or barrier semaphores. Data moves between devices by JAX's collectives and lax.ppermute only.
A program may use at most 64 MiB of HBM per device.

```python
import jax
import jax.numpy as jnp
from jax import lax

BLOCK = 128
PHYS_DIM = 16
RSEC = 2
LSEC = 4
TERMS = 16
ROWS = 512
COLS = 4096


def touch_ends(array, rng, smallest, largest):
    extent = array.shape
    spot = [jax.random.randint(jax.random.fold_in(rng, axis), (), 0, extent[axis]) for axis in range(len(extent))]
    array = array.at[tuple(spot)].set(smallest)
    longest = extent.index(max(extent))
    spot[longest] = (spot[longest] + 1) % extent[longest]
    return array.at[tuple(spot)].set(largest)


def steps_of(rng, extent, split, smallest, top_value):
    gain = 1.0
    for dim, blocks in split:
        steps = jax.random.uniform(jax.random.fold_in(jax.random.fold_in(rng, 6), dim), (blocks,), jnp.float32, smallest / len(split), top_value / len(split))
        gain = gain * jnp.repeat(jnp.exp(steps), extent[dim] // blocks).reshape((-1,) + (1,) * (len(extent) - 1 - dim))
    return gain


def noise(stream_key, shape, deviation, limit, cuts=(), dtype=jnp.bfloat16):
    result = jax.random.normal(stream_key, shape, jnp.float32) * deviation
    if len(cuts) > 0:
        result = steps_of(stream_key, shape, cuts, -0.22, 0.18) * result
    return jnp.clip(result, min=-limit, max=limit).astype(dtype)


def setup_inputs(seed: int = 0, part: int = 0) -> dict:
    key_list = jax.random.split(jax.random.key(seed), 8)
    own_keys = jax.random.split(jax.random.fold_in(key_list[7], part), 8)
    return {
        "wavefunction": noise(own_keys[0], (ROWS, COLS), 1.0, 6.0, ((1, 4),)),
        "left_blocks": noise(own_keys[1], (TERMS, LSEC, BLOCK, BLOCK), (BLOCK * TERMS) ** -0.5, 0.125, ((0, 4), (1, 4))),
        "right_blocks": noise(own_keys[2], (TERMS, RSEC, BLOCK, BLOCK), BLOCK ** -0.5, 0.5, ((0, 4),)),
        "site_terms": noise(own_keys[3], (TERMS, PHYS_DIM, PHYS_DIM), PHYS_DIM ** -0.5, 1.5, ((0, 4),)),
        "left_source": touch_ends(jax.random.randint(own_keys[4], (TERMS, LSEC), 0, LSEC), jax.random.fold_in(own_keys[4], 1), 0, LSEC - 1).astype(jnp.int32),
        "right_source": touch_ends(jax.random.randint(own_keys[5], (TERMS, RSEC), 0, RSEC), jax.random.fold_in(own_keys[5], 1), 0, RSEC - 1).astype(jnp.int32),
        "live_pairs": touch_ends((jax.random.randint(own_keys[6], (LSEC, RSEC), 0, 4) < 3).astype(jnp.int32), jax.random.fold_in(own_keys[6], 1), 0, 1),
    }


def term_sigma(wavefunction, left_one, right_one, site_one, left_one_source, right_one_source):
    whole_blocks = wavefunction.reshape(LSEC, BLOCK, COLS)
    source_rows = jnp.take(whole_blocks, left_one_source, axis=0)
    carried = jnp.einsum('aij,ajc->aic', left_one.astype(jnp.float32), source_rows.astype(jnp.float32)).astype(jnp.bfloat16)
    shaped = carried.reshape(ROWS, PHYS_DIM, RSEC, BLOCK)
    turned = jnp.einsum('st,itrj->isrj', site_one.astype(jnp.float32), shaped.astype(jnp.float32)).astype(jnp.bfloat16)
    picked = jnp.take(turned, right_one_source, axis=2)
    return jnp.einsum('isbj,bkj->isbk', picked.astype(jnp.float32), right_one.astype(jnp.float32))


def reference(wavefunction, left_blocks, right_blocks, site_terms, left_source, right_source, live_pairs):
    def advance(running, members):
        left_one, right_one, site_one, left_one_source, right_one_source = members
        return running + term_sigma(wavefunction, left_one, right_one, site_one, left_one_source, right_one_source), None

    start_value = jnp.zeros((ROWS, PHYS_DIM, RSEC, BLOCK), jnp.float32)
    running, _ = lax.scan(advance, start_value, (left_blocks, right_blocks, site_terms, left_source, right_source))
    row_mask = jnp.repeat(live_pairs.astype(jnp.float32), BLOCK, axis=0)
    running = running * row_mask[:, None, :, None]
    return running.reshape(ROWS, COLS).astype(jnp.bfloat16)
```

```python
import functools

import jax
import jax.numpy as jnp
from jax import lax
from jax.experimental import pallas as pl
from jax.experimental.pallas import tpu as pltpu
from jax.sharding import PartitionSpec as P

F32 = jnp.float32
BF16 = jnp.bfloat16
VMEM_BYTES = 32 * 1024 * 1024
NEAR = ((0, 1), (1, 0), (2, 3), (3, 2))
FAR = ((0, 2), (2, 0), (1, 3), (3, 1))
MIDDLE = ((1, 2), (2, 1))
OUTWARD = ((1, 0), (2, 3))
CORE = ((0, 1), (1, 0), (2, 3), (3, 2))
ACROSS = ((0, 2), (2, 0), (1, 3), (3, 1))
SUB = 16


def carry_left(blocks, sources, pieces):
    picked = jnp.take(blocks, sources, axis=0)
    return jnp.einsum(
        "...aij,...ajc->...aic", pieces, picked, preferred_element_type=F32
    ).astype(BF16)


def apply_right(received, site_one, source_one, right_one, physical, right_count, block_rows):
    shaped = received.reshape(received.shape[0], physical, right_count, block_rows)
    turned = jnp.einsum(
        "st,itrj->isrj", site_one, shaped, preferred_element_type=F32
    ).astype(BF16)
    picked = jnp.take(turned, source_one, axis=2)
    return jnp.einsum("isbj,bkj->isbk", picked, right_one, preferred_element_type=F32)


def by_terms(
    wavefunction, left_blocks, right_blocks, site_terms, left_source, right_source, live_pairs
):
    all_rows, columns = wavefunction.shape
    term_count, own_sectors, block_rows = left_blocks.shape[:3]
    physical = site_terms.shape[1]
    right_count = right_blocks.shape[1]
    own_rows = own_sectors * block_rows
    blocks = wavefunction.reshape(all_rows // block_rows, block_rows, columns)
    accumulated = jnp.zeros((own_rows, physical, right_count, block_rows), F32)
    for member in range(term_count):
        pieces = lax.all_gather(left_blocks[member], "blk", axis=0, tiled=True)
        carried = carry_left(blocks, left_source[member], pieces)
        received = lax.all_to_all(
            carried.reshape(all_rows, columns), "blk", split_axis=0, concat_axis=1, tiled=True
        )
        accumulated = accumulated + apply_right(
            received,
            site_terms[member],
            right_source[member],
            right_blocks[member],
            physical,
            right_count,
            block_rows,
        )
    position = lax.axis_index("blk")
    live_rows = lax.dynamic_slice_in_dim(live_pairs, position * own_sectors, own_sectors, 0)
    row_mask = jnp.repeat(live_rows.astype(F32), block_rows, axis=0)
    accumulated = accumulated * row_mask[:, None, :, None]
    flattened = accumulated.reshape(own_rows, physical * right_count * block_rows)
    summed = lax.psum_scatter(flattened, "mpo", scatter_dimension=1, tiled=True)
    return summed.astype(BF16)


def matmul(a, b):
    return jnp.dot(a, b, preferred_element_type=F32)


def pack_body(terms, rights, phys, place_ref, left_ref, right_ref, site_ref, sources_ref, rsource_ref, out_ref):
    block = left_ref.shape[-1]
    base = 0
    for w in range(terms):
        out_ref[base : base + block, :] = left_ref[w, 0]
        base += block
    for w in range(terms):
        for b in range(rights):
            out_ref[base : base + block, :] = right_ref[w, b]
            base += block
    lane = lax.broadcasted_iota(jnp.int32, (phys, block), 1)
    row = lax.broadcasted_iota(jnp.int32, (phys, block), 0)
    site = jnp.zeros((phys, block), F32)
    for w in range(terms):
        spot = jnp.where(lane == row + w * phys, 1.0, 0.0).astype(BF16)
        site = site + matmul(site_ref[w], spot)
    out_ref[base : base + phys, :] = site.astype(BF16)
    base += phys
    lane = lax.broadcasted_iota(jnp.int32, (SUB, block), 1)
    numbers = jnp.zeros((SUB, block), F32)
    for w in range(terms):
        numbers = jnp.where(lane == w, sources_ref[w, place_ref[1]].astype(F32), numbers)
        for b in range(rights):
            numbers = jnp.where(
                lane == terms + w * rights + b, rsource_ref[w, b].astype(F32), numbers
            )
    out_ref[base : base + SUB, :] = numbers.astype(BF16)


def operators(terms, rights, phys, place_ref, index_ref, live_ref, packs, w_ref, kron_ref):
    block = packs[0].shape[-1]
    per_term = 1 + rights
    me, own_blk = place_ref[0], place_ref[1]
    slots = len(packs)
    width = w_ref.shape[-1]
    for k in range(slots):
        for w in range(terms):
            for b in range(rights):
                start = (terms + w * rights + b) * block
                turned = packs[k][start : start + block, :].astype(F32).T.astype(BF16)
                source = index_ref[k, terms + w * rights + b]
                alive = live_ref[own_blk, b]
                for r in range(rights):
                    keep = jnp.logical_and(source == r, alive != 0)
                    w_ref[k * terms + w, r * block : (r + 1) * block, b * block : (b + 1) * block] = (
                        jnp.where(keep, turned, jnp.zeros_like(turned))
                    )
    site_at = per_term * terms * block
    site = jnp.concatenate([p[site_at : site_at + phys, :] for p in packs], axis=1)
    rows, depth = kron_ref.shape[1:]
    quarter = phys // slots
    srow = lax.broadcasted_iota(jnp.int32, (rows, phys), 0) // SUB
    owner = jnp.where(srow < quarter, lax.bitwise_xor(me, 2), me)
    swant = owner * quarter + lax.rem(srow, quarter)
    pick_s = jnp.where(
        lax.broadcasted_iota(jnp.int32, (rows, phys), 1) == swant, 1.0, 0.0
    ).astype(BF16)
    here = slots * block
    source_row = lax.broadcasted_iota(jnp.int32, (here, depth), 0)
    column = lax.broadcasted_iota(jnp.int32, (here, depth), 1)
    want_term = column // (2 * SUB)
    which = lax.rem(column // SUB, 2)
    diagonal = lax.rem(lax.broadcasted_iota(jnp.int32, (rows, depth), 0), SUB) == lax.rem(
        lax.broadcasted_iota(jnp.int32, (rows, depth), 1), SUB
    )
    per_blk = slots
    for q in range(slots):
        state = lax.bitwise_xor(own_blk, q) * per_blk + lax.bitwise_xor(me, which)
        want = (want_term // terms) * block + lax.rem(want_term, terms) * phys + state
        pick_t = jnp.where(source_row == want, 1.0, 0.0).astype(BF16)
        spread = matmul(pick_s, matmul(site, pick_t).astype(BF16))
        kron_ref[q] = jnp.where(diagonal, spread, 0.0).astype(BF16)


def add_shard(terms, index_ref, packs, w_ref, kron, halves, y_ref):
    block = packs[0].shape[-1]
    tiles = y_ref.shape[0]
    for k in range(len(packs)):
        for w in range(terms):
            row = pl.multiple_of(index_ref[k, w] * block, block)
            left = packs[k][w * block : (w + 1) * block, :]
            carried = jnp.concatenate(
                [matmul(left, h[pl.ds(row, block), :]).astype(BF16) for h in halves], axis=0
            )
            y = matmul(carried, w_ref[k * terms + w]).astype(BF16)
            at = (k * terms + w) * 2 * SUB
            for t in range(2):
                y_ref[:, at + t * SUB : at + (t + 1) * SUB, :] = y[
                    t * block : (t + 1) * block, :
                ].reshape(tiles, SUB, y.shape[-1])
    return [matmul(kron, y_ref[i]) for i in range(tiles)]


def own_body(terms, rights, phys, place_ref, index_ref, live_ref, *refs):
    packs, (mine, other), (w_ref, kron_ref, acc_ref), (y_ref,) = (
        refs[:4], refs[4:6], refs[6:9], refs[9:])
    operators(terms, rights, phys, place_ref, index_ref, live_ref, packs, w_ref, kron_ref)
    sums = add_shard(terms, index_ref, packs, w_ref, kron_ref[0], (mine, other), y_ref)
    for i, s in enumerate(sums):
        acc_ref[i] = s


def middle_body(terms, index_ref, *refs):
    packs, w_ref, kron_ref, acc_in, near, far = refs[:4], refs[4], refs[5], refs[6], refs[7:9], refs[9:11]
    acc_ref, y_ref = refs[11], refs[12]
    for q, halves in ((1, near), (2, far)):
        sums = add_shard(terms, index_ref, packs, w_ref, kron_ref[q], halves, y_ref)
        for i, s in enumerate(sums):
            acc_ref[i] = s + (acc_in[i] if q == 1 else acc_ref[i])


def last_body(terms, place_ref, index_ref, *refs):
    packs, w_ref, kron_ref, acc_in = refs[:4], refs[4], refs[5], refs[6]
    inner, outer = refs[7:9], refs[9:11]
    give_ref, keep_ref, y_ref, half_ref = refs[11:]
    at_end = jnp.logical_or(place_ref[1] == 0, place_ref[1] == 3)
    for h in range(2):
        half_ref[h] = jnp.where(at_end, outer[h][...], inner[h][...])
    sums = add_shard(
        terms, index_ref, packs, w_ref, kron_ref[3], (half_ref.at[0], half_ref.at[1]), y_ref
    )
    width = w_ref.shape[-1]
    for i, s in enumerate(sums):
        total = s + acc_in[i]
        count = total.shape[0] // SUB // 2
        for n in range(count):
            rows, cols = slice(i * SUB, (i + 1) * SUB), slice(n * width, (n + 1) * width)
            give_ref[rows, cols] = total[n * SUB : (n + 1) * SUB, :].astype(BF16)
            keep_ref[rows, cols] = total[(count + n) * SUB : (count + n + 1) * SUB, :]


def call(body, out_shape, in_specs, scratch=(), flops=0, nbytes=0, name=None):
    return pl.pallas_call(
        body,
        out_shape=out_shape,
        in_specs=in_specs,
        scratch_shapes=scratch,
        compiler_params=pltpu.CompilerParams(vmem_limit_bytes=VMEM_BYTES),
        cost_estimate=pl.CostEstimate(flops=flops, bytes_accessed=nbytes, transcendentals=0),
        name=name,
    )


def by_states(
    wavefunction, left_blocks, right_blocks, site_terms, left_source, right_source, live_pairs
):
    all_rows, columns = wavefunction.shape
    terms, _, block, _ = left_blocks.shape
    rights = right_blocks.shape[1]
    phys = site_terms.shape[1]
    width = rights * block
    slots = 4
    depth = slots * terms * 2 * SUB
    rows = phys // 2 * SUB
    tiles = block // SUB
    me, own_blk = lax.axis_index("mpo"), lax.axis_index("blk")
    place = jnp.stack([me, own_blk]).astype(jnp.int32)
    smem = pl.BlockSpec(memory_space=pltpu.SMEM)
    vmem = pl.BlockSpec(memory_space=pltpu.VMEM)

    mine = lax.dynamic_slice_in_dim(wavefunction, me * width, width, 1)
    far = lax.ppermute(mine, "blk", FAR)
    near = lax.ppermute(mine, "blk", NEAR)
    inner = lax.ppermute(mine, "blk", MIDDLE)
    outer = lax.ppermute(far, "blk", OUTWARD)

    pack_rows = terms * (1 + rights) * block + phys + SUB
    pack = call(
        functools.partial(pack_body, terms, rights, phys),
        jax.ShapeDtypeStruct((pack_rows, block), BF16),
        [smem, vmem, vmem, vmem, smem, smem],
        name="pack_operators",
    )(place, left_blocks, right_blocks, site_terms, left_source, right_source)
    pack_x = lax.ppermute(pack, "mpo", ACROSS)
    pack_c = lax.ppermute(pack, "mpo", CORE)
    pack_xc = lax.ppermute(pack_x, "mpo", CORE)
    packs = (pack, pack_x, pack_c, pack_xc)
    numbers = terms * (1 + rights)
    index = jnp.stack([p[pack_rows - SUB, :numbers] for p in packs]).astype(jnp.int32)

    def swap(x):
        return lax.ppermute(x, "mpo", CORE)

    other = lax.dynamic_slice_in_dim(wavefunction, lax.bitwise_xor(me, 1) * width, width, 1)
    shard_flops = 2 * slots * terms * (2 * block * width * (block + width)) + 2 * tiles * rows * depth * width
    y_scratch = pltpu.VMEM((tiles, depth, width), BF16)
    acc_shape = jax.ShapeDtypeStruct((tiles, rows, width), F32)
    w_all, kron, acc = call(
        functools.partial(own_body, terms, rights, phys),
        (
            jax.ShapeDtypeStruct((slots * terms, width, width), BF16),
            jax.ShapeDtypeStruct((slots, rows, depth), BF16),
            acc_shape,
        ),
        [smem, smem, smem] + [vmem] * 6,
        [y_scratch],
        flops=shard_flops,
        nbytes=8 << 20,
        name="own_shard",
    )(place, index, live_pairs, *packs, mine, other)
    acc = call(
        functools.partial(middle_body, terms),
        acc_shape,
        [smem] + [vmem] * 11,
        [y_scratch],
        flops=2 * shard_flops,
        nbytes=8 << 20,
        name="middle_shards",
    )(index, *packs, w_all, kron, acc, near, swap(near), far, swap(far))
    give, keep = call(
        functools.partial(last_body, terms),
        (
            jax.ShapeDtypeStruct((block, phys // slots * width), BF16),
            jax.ShapeDtypeStruct((block, phys // slots * width), F32),
        ),
        [smem, smem] + [vmem] * 11,
        [y_scratch, pltpu.VMEM((2, all_rows, width), BF16)],
        flops=shard_flops,
        nbytes=8 << 20,
        name="last_shard",
    )(place, index, *packs, w_all, kron, acc, inner, swap(inner), outer, swap(outer))
    taken = lax.ppermute(give, "mpo", ACROSS)
    return (keep + taken.astype(F32)).astype(BF16)


def solution(mesh):
    sizes = dict(mesh.shape)

    def on_device(
        wavefunction, left_blocks, right_blocks, site_terms, left_source, right_source, live_pairs
    ):
        columns = wavefunction.shape[1]
        terms, sectors, block, _ = left_blocks.shape
        phys, rights = site_terms.shape[1], right_blocks.shape[1]
        square = sizes["blk"] == 4 and sizes["mpo"] == 4 and sectors == 1 and rights == 2
        fits = columns == 4 * rights * block and phys == 16 and block == 128 and terms == 4
        step = by_states if square and fits else by_terms
        return step(
            wavefunction, left_blocks, right_blocks, site_terms, left_source, right_source, live_pairs
        )

    return jax.shard_map(
        on_device,
        mesh=mesh,
        in_specs=(
            P("rep", "blk"),
            P(("rep", "mpo"), "blk", None, None),
            P(("rep", "mpo"), None, None, None),
            P(("rep", "mpo"), None, None),
            P(("rep", "mpo"), None),
            P(("rep", "mpo"), None),
            P("rep", None),
        ),
        out_specs=P(("rep", "blk"), "mpo"),
        check_vma=False,
    )
```

```python
import functools

import jax
import jax.numpy as jnp
from jax import lax
from jax.experimental import pallas as pl
from jax.experimental.pallas import tpu as pltpu
from jax.sharding import PartitionSpec as P

F32 = jnp.float32
BF16 = jnp.bfloat16
VMEM_BYTES = 32 * 1024 * 1024
SLICE_BYTES = 53 * 1024 * 1024
PACK_BYTES = 53 * 1024 * 1024
CHIP_FLOPS = int(8e9)
CORE_FLOPS = int(3e9)
NEAR = ((0, 1), (1, 0), (2, 3), (3, 2))
FAR = ((0, 2), (2, 0), (1, 3), (3, 1))
MIDDLE = ((1, 2), (2, 1))
OUTWARD = ((1, 0), (2, 3))
CORE = ((0, 1), (1, 0), (2, 3), (3, 2))
ACROSS = ((0, 2), (2, 0), (1, 3), (3, 1))
SUB = 16


def carry_left(blocks, sources, pieces):
    picked = jnp.take(blocks, sources, axis=0)
    return jnp.einsum(
        "...aij,...ajc->...aic", pieces, picked, preferred_element_type=F32
    ).astype(BF16)


def apply_right(received, site_one, source_one, right_one, physical, right_count, block_rows):
    shaped = received.reshape(received.shape[0], physical, right_count, block_rows)
    turned = jnp.einsum(
        "st,itrj->isrj", site_one, shaped, preferred_element_type=F32
    ).astype(BF16)
    picked = jnp.take(turned, source_one, axis=2)
    return jnp.einsum("isbj,bkj->isbk", picked, right_one, preferred_element_type=F32)


def by_terms(
    wavefunction, left_blocks, right_blocks, site_terms, left_source, right_source, live_pairs
):
    all_rows, columns = wavefunction.shape
    term_count, own_sectors, block_rows = left_blocks.shape[:3]
    physical = site_terms.shape[1]
    right_count = right_blocks.shape[1]
    own_rows = own_sectors * block_rows
    blocks = wavefunction.reshape(all_rows // block_rows, block_rows, columns)
    accumulated = jnp.zeros((own_rows, physical, right_count, block_rows), F32)
    for member in range(term_count):
        pieces = lax.all_gather(left_blocks[member], "blk", axis=0, tiled=True)
        carried = carry_left(blocks, left_source[member], pieces)
        received = lax.all_to_all(
            carried.reshape(all_rows, columns), "blk", split_axis=0, concat_axis=1, tiled=True
        )
        accumulated = accumulated + apply_right(
            received,
            site_terms[member],
            right_source[member],
            right_blocks[member],
            physical,
            right_count,
            block_rows,
        )
    position = lax.axis_index("blk")
    live_rows = lax.dynamic_slice_in_dim(live_pairs, position * own_sectors, own_sectors, 0)
    row_mask = jnp.repeat(live_rows.astype(F32), block_rows, axis=0)
    accumulated = accumulated * row_mask[:, None, :, None]
    flattened = accumulated.reshape(own_rows, physical * right_count * block_rows)
    summed = lax.psum_scatter(flattened, "mpo", scatter_dimension=1, tiled=True)
    return summed.astype(BF16)


def matmul(a, b):
    return jnp.dot(a, b, preferred_element_type=F32)


def slice_body(wave_ref, own_ref, sem):
    width = own_ref.shape[1]
    start = pl.multiple_of(lax.axis_index("mpo") * width, width)
    copy = pltpu.make_async_copy(wave_ref.at[:, pl.ds(start, width)], own_ref, sem)
    copy.start()
    copy.wait()


def pack_body(
    terms, rights, phys, left_hbm, right_hbm, site_hbm, sources_hbm, rsource_hbm, live_hbm,
    pack_ref, right_ref, site_ref, sources_ref, rsource_ref, live_ref, sems,
):
    block = right_ref.shape[-1]
    own_blk = lax.axis_index("blk")
    inputs = [
        (right_hbm, right_ref),
        (site_hbm, site_ref),
        (sources_hbm, sources_ref),
        (rsource_hbm, rsource_ref),
        (live_hbm, live_ref),
    ]
    for w in range(terms):
        inputs.append((left_hbm.at[w, 0], pack_ref.at[pl.ds(w * block, block), :]))
    copies = [
        pltpu.make_async_copy(source, target, sems.at[n])
        for n, (source, target) in enumerate(inputs)
    ]
    for copy in copies:
        copy.start()
    for copy in copies[1:5]:
        copy.wait()
    base = terms * (1 + rights) * block
    lane = lax.broadcasted_iota(jnp.int32, (phys, block), 1)
    row = lax.broadcasted_iota(jnp.int32, (phys, block), 0)
    site = jnp.zeros((phys, block), F32)
    for w in range(terms):
        spot = jnp.where(lane == row + w * phys, 1.0, 0.0).astype(BF16)
        site = site + matmul(site_ref[w], spot)
    pack_ref[base : base + phys, :] = site.astype(BF16)
    numbers = jnp.zeros((SUB, block), F32)
    lane = lax.broadcasted_iota(jnp.int32, (SUB, block), 1)
    for w in range(terms):
        numbers = jnp.where(lane == w, sources_ref[w, own_blk].astype(F32), numbers)
        for b in range(rights):
            at = terms + w * rights + b
            numbers = jnp.where(lane == at, rsource_ref[b, w].astype(F32), numbers)
    for b in range(rights):
        at = terms * (1 + rights) + b
        numbers = jnp.where(lane == at, live_ref[b, own_blk].astype(F32), numbers)
    pack_ref[base + phys : base + phys + SUB, :] = numbers.astype(BF16)
    copies[0].wait()
    for w in range(terms):
        for b in range(rights):
            at = (terms + w * rights + b) * block
            pack_ref[at : at + block, :] = right_ref[w, b].astype(F32).T.astype(BF16)
    for copy in copies[5:]:
        copy.wait()


def right_matrices(terms, rights, numbers, alive, packs, w_ref):
    block = packs[0].shape[-1]
    for k in range(len(packs)):
        for w in range(terms):
            for b in range(rights):
                start = (terms + w * rights + b) * block
                turned = packs[k][start : start + block, :]
                source = numbers[k, terms + w * rights + b]
                for r in range(rights):
                    keep = jnp.logical_and(source == r, alive[b] != 0)
                    w_ref[k * terms + w, r * block : (r + 1) * block, b * block : (b + 1) * block] = (
                        jnp.where(keep, turned, jnp.zeros_like(turned))
                    )


def spread_site(terms, rights, phys, packs, first, kron_ref):
    block = packs[0].shape[-1]
    me, own_blk = lax.axis_index("mpo"), lax.axis_index("blk")
    site_at = (1 + rights) * terms * block
    site = jnp.concatenate([p[site_at : site_at + phys, :] for p in packs], axis=1)
    rows, depth = kron_ref.shape
    quarter, here = phys // 4, len(packs) * block
    srow = lax.broadcasted_iota(jnp.int32, (rows, phys), 0) >> 4
    turn = srow >> 2
    owner = lax.bitwise_xor(me, jnp.where(turn == 0, 3, jnp.where(turn == 3, 0, turn)))
    swant = owner * quarter + (srow & 3)
    pick_s = jnp.where(
        lax.broadcasted_iota(jnp.int32, (rows, phys), 1) == swant, 1.0, 0.0
    ).astype(BF16)
    column = lax.broadcasted_iota(jnp.int32, (here, depth), 1)
    slot = column >> 4
    shard, pack, term = slot // (terms * len(packs)), (slot // terms) % len(packs), slot % terms
    state = lax.bitwise_xor(own_blk, shard + first) * quarter + me
    pick_t = jnp.where(
        lax.broadcasted_iota(jnp.int32, (here, depth), 0) == pack * block + term * phys + state,
        1.0,
        0.0,
    ).astype(BF16)
    spread = matmul(pick_s, matmul(site, pick_t).astype(BF16))
    diagonal = (lax.broadcasted_iota(jnp.int32, (rows, depth), 0) & 15) == (
        lax.broadcasted_iota(jnp.int32, (rows, depth), 1) & 15
    )
    kron_ref[...] = jnp.where(diagonal, spread, 0.0).astype(BF16)


def turn_shard(terms, numbers, packs, w_ref, shard, y_ref, at):
    block = packs[0].shape[-1]
    tiles = y_ref.shape[0]
    for k in range(len(packs)):
        for w in range(terms):
            row = pl.multiple_of(numbers[k, w] * block, block)
            left = packs[k][w * block : (w + 1) * block, :]
            carried = matmul(left, shard[pl.ds(row, block), :]).astype(BF16)
            y = matmul(carried, w_ref[k * terms + w]).astype(BF16)
            y_ref[:, at : at + SUB, :] = y.reshape(tiles, SUB, y.shape[-1])
            at += SUB
    return at


class Numbers:
    def __init__(self, refs):
        self.refs = refs

    def __getitem__(self, at):
        return self.refs[at[0]][0, at[1]]


def terms_body(terms, rights, phys, plan, live_ref, *refs):
    packs_n, shards_n, first, make, before, all_n = plan
    number_refs, refs = refs[:packs_n], refs[packs_n:]
    packs, refs = refs[:packs_n], refs[packs_n:]
    others, refs = refs[:all_n], refs[all_n:]
    shards, refs = refs[:shards_n], refs[shards_n:]
    if not make:
        w_ref, refs = refs[0], refs[1:]
    acc_in, refs = (refs[0], refs[1:]) if before else (None, refs)
    numbers = Numbers(number_refs)
    if make:
        w_ref, refs = refs[0], refs[1:]
        alive = [live_ref[0, terms * (1 + rights) + b] for b in range(rights)]
        right_matrices(terms, rights, numbers, alive, packs, w_ref)
    if all_n:
        spread_site(terms, rights, phys, others, 3, refs[0])
        refs = refs[1:]
    acc_ref, kron_ref, y_ref = refs
    spread_site(terms, rights, phys, packs, first, kron_ref)
    at = 0
    for shard in shards:
        at = turn_shard(terms, numbers, packs, w_ref, shard, y_ref, at)
    for i in range(y_ref.shape[0]):
        total = matmul(kron_ref[...], y_ref[i])
        acc_ref[i] = total if acc_in is None else total + acc_in[i]


def last_body(terms, *refs):
    number_refs, packs, (w_own, w_core, w_far, kron_ref, acc_in) = refs[:4], refs[4:8], refs[8:13]
    inner, outer = refs[13:15]
    quarters, (y_ref, shard_ref) = refs[15:19], refs[19:]
    own_blk = lax.axis_index("blk")
    at_end = jnp.logical_or(own_blk == 0, own_blk == 3)
    shard_ref[...] = jnp.where(at_end, outer[...], inner[...])
    at = 0
    for here, w_ref in (((0,), w_own), ((1,), w_core), ((2, 3), w_far)):
        numbers = Numbers([number_refs[k] for k in here])
        at = turn_shard(terms, numbers, [packs[k] for k in here], w_ref, shard_ref, y_ref, at)
    width = w_own.shape[-1]
    for i in range(y_ref.shape[0]):
        total = matmul(kron_ref[...], y_ref[i]) + acc_in[i]
        count = total.shape[0] // SUB // 4
        for n, target in enumerate(quarters):
            for m in range(count):
                start = (n * count + m) * SUB
                target[i * SUB : (i + 1) * SUB, m * width : (m + 1) * width] = total[
                    start : start + SUB, :
                ].astype(target.dtype)


def call(body, out_shape, in_specs, scratch=(), out_specs=None, name=None, vmem=VMEM_BYTES, flops=1000):
    extra = {} if out_specs is None else {"out_specs": out_specs}
    return pl.pallas_call(
        body,
        out_shape=out_shape,
        in_specs=in_specs,
        scratch_shapes=scratch,
        compiler_params=pltpu.CompilerParams(vmem_limit_bytes=vmem),
        cost_estimate=pl.CostEstimate(flops=flops, bytes_accessed=1000, transcendentals=0),
        name=name,
        **extra,
    )


def by_states(
    wavefunction, left_blocks, right_blocks, site_terms, left_source, right_source, live_pairs
):
    all_rows = wavefunction.shape[0]
    terms, _, block, _ = left_blocks.shape
    rights = right_blocks.shape[1]
    phys = site_terms.shape[1]
    width = rights * block
    slots = 4
    rows = phys * SUB
    tiles = block // SUB
    smem = pl.BlockSpec(memory_space=pltpu.SMEM)
    vmem = pl.BlockSpec(memory_space=pltpu.VMEM)
    hbm = pl.BlockSpec(memory_space=pltpu.HBM)

    pack_rows = terms * (1 + rights) * block + phys + SUB
    mine = call(
        slice_body,
        jax.ShapeDtypeStruct((all_rows, width), BF16),
        [hbm],
        [pltpu.SemaphoreType.DMA],
        out_specs=vmem,
        name="own_states",
        vmem=SLICE_BYTES,
    )(wavefunction)

    def swap(x):
        return lax.ppermute(x, "mpo", CORE)

    pack = call(
        functools.partial(pack_body, terms, rights, phys),
        jax.ShapeDtypeStruct((pack_rows, block), BF16),
        [hbm] * 6,
        [
            pltpu.VMEM(right_blocks.shape, BF16),
            pltpu.VMEM(site_terms.shape, BF16),
            pltpu.SMEM(left_source.shape, jnp.int32),
            pltpu.SMEM(right_source.T.shape, jnp.int32),
            pltpu.SMEM(live_pairs.T.shape, jnp.int32),
            pltpu.SemaphoreType.DMA((terms + 5,)),
        ],
        out_specs=vmem,
        name="pack_operators",
        vmem=PACK_BYTES,
    )(left_blocks, right_blocks, site_terms, left_source, right_source.T, live_pairs.T)

    def numbers_of(p):
        return p[pack_rows - SUB : pack_rows - SUB + 1, :].astype(jnp.int32)

    far = lax.ppermute(mine, "blk", FAR)
    near = lax.ppermute(mine, "blk", NEAR)
    pack_x = lax.ppermute(pack, "mpo", ACROSS)
    acc_shape = jax.ShapeDtypeStruct((tiles, rows, width), F32)
    one_pack = terms * SUB

    def run(name, packs, numbers, shards, first, acc, w=None, every=(), flops=1000):
        plan = (len(packs), len(shards), first, w is None, acc is not None, len(every))
        depth = len(packs) * len(shards) * one_pack
        shapes = [acc_shape]
        if every:
            shapes.insert(0, jax.ShapeDtypeStruct((rows, len(every) * one_pack), BF16))
        if w is None:
            shapes.insert(0, jax.ShapeDtypeStruct((len(packs) * terms, width, width), BF16))
        arrays = [*packs, *every, *shards]
        arrays += [a for a in (w, acc) if a is not None]
        return call(
            functools.partial(terms_body, terms, rights, phys, plan),
            tuple(shapes),
            [smem] * (1 + len(numbers)) + [vmem] * len(arrays),
            [pltpu.VMEM((rows, depth), BF16), pltpu.VMEM((tiles, depth, width), BF16)],
            name=name,
            flops=flops,
        )(own_number, *numbers, *arrays)

    own_number = numbers_of(pack)
    w_own, acc = run("own_terms_own", (pack,), (own_number,), (mine,), 0, None)
    far, acc = lax.optimization_barrier((far, acc))
    outer = lax.ppermute(far, "blk", OUTWARD)
    far, later, pack_own = lax.optimization_barrier((far, mine, pack))
    inner = lax.ppermute(later, "blk", MIDDLE)
    pack_c = swap(pack_own)
    (acc,) = run(
        "own_terms", (pack_own,), (own_number,), (near, far), 1, acc, w=w_own, flops=CHIP_FLOPS
    )
    acc, pack_x, pack_c = lax.optimization_barrier((acc, pack_x, pack_c))
    core_number = numbers_of(pack_c)
    x_packs = (pack_x, swap(pack_x))
    x_numbers = [numbers_of(p) for p in x_packs]
    w_core, acc = run(
        "core_terms", (pack_c,), (core_number,), (later, near, far), 0, acc, flops=CORE_FLOPS
    )
    packs = (pack_own, pack_c, *x_packs)
    w_far, kron, acc = run(
        "beside_terms", x_packs, x_numbers, (later, near, far), 0, acc, every=packs
    )
    outer, acc = lax.optimization_barrier((outer, acc))
    quarter = (block, phys // slots * width)
    give_far, give_core, keep_x, keep = call(
        functools.partial(last_body, terms),
        tuple(jax.ShapeDtypeStruct(quarter, t) for t in (BF16, BF16, F32, F32)),
        [smem] * 4 + [vmem] * 11,
        [pltpu.VMEM((tiles, slots * one_pack, width), BF16), pltpu.VMEM((all_rows, width), BF16)],
        name="last_shard",
    )(
        own_number, core_number, *x_numbers, *packs, w_own, w_core, w_far, kron, acc, inner, outer
    )
    give = (keep_x + swap(give_far).astype(F32)).astype(BF16)
    taken = lax.ppermute(give, "mpo", ACROSS)
    return (keep + swap(give_core).astype(F32) + taken.astype(F32)).astype(BF16)


def solution(mesh):
    sizes = dict(mesh.shape)

    def on_device(
        wavefunction, left_blocks, right_blocks, site_terms, left_source, right_source, live_pairs
    ):
        columns = wavefunction.shape[1]
        terms, sectors, block, _ = left_blocks.shape
        phys, rights = site_terms.shape[1], right_blocks.shape[1]
        square = sizes["blk"] == 4 and sizes["mpo"] == 4 and sectors == 1 and rights == 2
        fits = columns == 4 * rights * block and phys == 16 and block == 128 and terms == 4
        step = by_states if square and fits else by_terms
        return step(
            wavefunction, left_blocks, right_blocks, site_terms, left_source, right_source, live_pairs
        )

    return jax.shard_map(
        on_device,
        mesh=mesh,
        in_specs=(
            P("rep", "blk"),
            P(("rep", "mpo"), "blk", None, None),
            P(("rep", "mpo"), None, None, None),
            P(("rep", "mpo"), None, None),
            P(("rep", "mpo"), None),
            P(("rep", "mpo"), None),
            P("rep", None),
        ),
        out_specs=P(("rep", "blk"), "mpo"),
        check_vma=False,
    )
```

```python
import functools

import jax
import jax.numpy as jnp
from jax import lax
from jax.experimental import pallas as pl
from jax.experimental.pallas import tpu as pltpu
from jax.sharding import PartitionSpec as P

F32 = jnp.float32
BF16 = jnp.bfloat16
VMEM_BYTES = 32 * 1024 * 1024
SLICE_BYTES = 32 * 1024 * 1024
PACK_BYTES = 32 * 1024 * 1024
OWN_FLOPS = 1000
CHIP_FLOPS = int(8e9)
OTHER_FLOPS = 1000
CORE_FLOPS = int(3e9)
NEAR = ((0, 1), (1, 0), (2, 3), (3, 2))
FAR = ((0, 2), (2, 0), (1, 3), (3, 1))
CORE = ((0, 1), (1, 0), (2, 3), (3, 2))
ACROSS = ((0, 2), (2, 0), (1, 3), (3, 1))
SUB = 16


def carry_left(blocks, sources, pieces):
    picked = jnp.take(blocks, sources, axis=0)
    return jnp.einsum(
        "...aij,...ajc->...aic", pieces, picked, preferred_element_type=F32
    ).astype(BF16)


def apply_right(received, site_one, source_one, right_one, physical, right_count, block_rows):
    shaped = received.reshape(received.shape[0], physical, right_count, block_rows)
    turned = jnp.einsum(
        "st,itrj->isrj", site_one, shaped, preferred_element_type=F32
    ).astype(BF16)
    picked = jnp.take(turned, source_one, axis=2)
    return jnp.einsum("isbj,bkj->isbk", picked, right_one, preferred_element_type=F32)


def by_terms(
    wavefunction, left_blocks, right_blocks, site_terms, left_source, right_source, live_pairs
):
    all_rows, columns = wavefunction.shape
    term_count, own_sectors, block_rows = left_blocks.shape[:3]
    physical = site_terms.shape[1]
    right_count = right_blocks.shape[1]
    own_rows = own_sectors * block_rows
    blocks = wavefunction.reshape(all_rows // block_rows, block_rows, columns)
    accumulated = jnp.zeros((own_rows, physical, right_count, block_rows), F32)
    for member in range(term_count):
        pieces = lax.all_gather(left_blocks[member], "blk", axis=0, tiled=True)
        carried = carry_left(blocks, left_source[member], pieces)
        received = lax.all_to_all(
            carried.reshape(all_rows, columns), "blk", split_axis=0, concat_axis=1, tiled=True
        )
        accumulated = accumulated + apply_right(
            received,
            site_terms[member],
            right_source[member],
            right_blocks[member],
            physical,
            right_count,
            block_rows,
        )
    position = lax.axis_index("blk")
    live_rows = lax.dynamic_slice_in_dim(live_pairs, position * own_sectors, own_sectors, 0)
    row_mask = jnp.repeat(live_rows.astype(F32), block_rows, axis=0)
    accumulated = accumulated * row_mask[:, None, :, None]
    flattened = accumulated.reshape(own_rows, physical * right_count * block_rows)
    summed = lax.psum_scatter(flattened, "mpo", scatter_dimension=1, tiled=True)
    return summed.astype(BF16)


def matmul(a, b):
    return jnp.dot(a, b, preferred_element_type=F32)


def slice_body(wave_ref, own_ref, sem):
    width = own_ref.shape[1]
    start = pl.multiple_of(lax.axis_index("mpo") * width, width)
    copy = pltpu.make_async_copy(wave_ref.at[:, pl.ds(start, width)], own_ref, sem)
    copy.start()
    copy.wait()


def pack_body(
    terms, rights, phys, left_hbm, right_hbm, site_hbm, sources_hbm, rsource_hbm, live_hbm,
    pack_ref, right_ref, site_ref, sources_ref, rsource_ref, live_ref, sems,
):
    block = right_ref.shape[-1]
    own_blk = lax.axis_index("blk")
    inputs = [
        (right_hbm, right_ref),
        (site_hbm, site_ref),
        (sources_hbm, sources_ref),
        (rsource_hbm, rsource_ref),
        (live_hbm, live_ref),
    ]
    for w in range(terms):
        inputs.append((left_hbm.at[w, 0], pack_ref.at[pl.ds(w * block, block), :]))
    copies = [
        pltpu.make_async_copy(source, target, sems.at[n])
        for n, (source, target) in enumerate(inputs)
    ]
    for copy in copies:
        copy.start()
    for copy in copies[1:5]:
        copy.wait()
    base = terms * (1 + rights) * block
    lane = lax.broadcasted_iota(jnp.int32, (phys, block), 1)
    row = lax.broadcasted_iota(jnp.int32, (phys, block), 0)
    site = jnp.zeros((phys, block), F32)
    for w in range(terms):
        spot = jnp.where(lane == row + w * phys, 1.0, 0.0).astype(BF16)
        site = site + matmul(site_ref[w], spot)
    pack_ref[base : base + phys, :] = site.astype(BF16)
    numbers = jnp.zeros((SUB, block), F32)
    lane = lax.broadcasted_iota(jnp.int32, (SUB, block), 1)
    for w in range(terms):
        numbers = jnp.where(lane == w, sources_ref[w, own_blk].astype(F32), numbers)
        for b in range(rights):
            at = terms + w * rights + b
            numbers = jnp.where(lane == at, rsource_ref[b, w].astype(F32), numbers)
    for b in range(rights):
        at = terms * (1 + rights) + b
        numbers = jnp.where(lane == at, live_ref[b, own_blk].astype(F32), numbers)
    pack_ref[base + phys : base + phys + SUB, :] = numbers.astype(BF16)
    copies[0].wait()
    for w in range(terms):
        for b in range(rights):
            at = (terms + w * rights + b) * block
            pack_ref[at : at + block, :] = right_ref[w, b].astype(F32).T.astype(BF16)
    for copy in copies[5:]:
        copy.wait()


def right_matrices(terms, rights, numbers, alive, pack, w_ref):
    block = pack.shape[-1]
    for w in range(terms):
        for b in range(rights):
            start = (terms + w * rights + b) * block
            turned = pack[start : start + block, :]
            source = numbers[0, terms + w * rights + b]
            for r in range(rights):
                keep = jnp.logical_and(source == r, alive[b] != 0)
                w_ref[w, r * block : (r + 1) * block, b * block : (b + 1) * block] = jnp.where(
                    keep, turned, jnp.zeros_like(turned)
                )


def spread_site(terms, rights, phys, packs, chunks, kron_ref):
    block = packs[0].shape[-1]
    me, own_blk = lax.axis_index("mpo"), lax.axis_index("blk")
    site_at = (1 + rights) * terms * block
    site = jnp.concatenate([p[site_at : site_at + phys, :] for p in packs], axis=1)
    rows, depth = kron_ref.shape
    quarter, here = phys // 4, len(packs) * block
    srow = lax.broadcasted_iota(jnp.int32, (rows, phys), 0) >> 4
    turn = srow >> 2
    owner = lax.bitwise_xor(me, jnp.where(turn == 0, 3, jnp.where(turn == 3, 0, turn)))
    swant = owner * quarter + (srow & 3)
    pick_s = jnp.where(
        lax.broadcasted_iota(jnp.int32, (rows, phys), 1) == swant, 1.0, 0.0
    ).astype(BF16)
    slot = lax.broadcasted_iota(jnp.int32, (1, depth), 1) >> 4
    want = jnp.zeros((1, depth), jnp.int32)
    for n, (shard, pack) in enumerate(chunks):
        state = lax.bitwise_xor(own_blk, shard) * quarter + me
        spot = pack * block + (slot - n * terms) * phys + state
        want = jnp.where(jnp.logical_and(slot >= n * terms, slot < (n + 1) * terms), spot, want)
    pick_t = jnp.where(
        lax.broadcasted_iota(jnp.int32, (here, depth), 0) == want, 1.0, 0.0
    ).astype(BF16)
    spread = matmul(pick_s, matmul(site, pick_t).astype(BF16))
    diagonal = (lax.broadcasted_iota(jnp.int32, (rows, depth), 0) & 15) == (
        lax.broadcasted_iota(jnp.int32, (rows, depth), 1) & 15
    )
    kron_ref[...] = jnp.where(diagonal, spread, 0.0).astype(BF16)


def turn_shard(terms, numbers, pack, w_ref, shard, y_ref, at):
    block = pack.shape[-1]
    tiles = y_ref.shape[0]
    for w in range(terms):
        row = pl.multiple_of(numbers[0, w] * block, block)
        left = pack[w * block : (w + 1) * block, :]
        carried = matmul(left, shard[pl.ds(row, block), :]).astype(BF16)
        y = matmul(carried, w_ref[w]).astype(BF16)
        y_ref[:, at + w * SUB : at + (w + 1) * SUB, :] = y.reshape(tiles, SUB, y.shape[-1])


class Plan:
    def __init__(self, packs, chunks, made=(), before=True, prepare_last=False, last=False):
        self.packs, self.chunks, self.made = packs, chunks, made
        self.before, self.prepare_last, self.last = before, prepare_last, last
        self.used = sorted({k for _, k in chunks})
        self.given = [k for k in self.used if k not in made]
        self.shards = sorted({q for q, _ in chunks})


def terms_body(terms, rights, phys, plan, live_ref, *refs):
    refs = list(refs)

    def take(count):
        taken, refs[:] = refs[:count], refs[count:]
        return taken

    numbers, packs = take(plan.packs), take(plan.packs)
    w_refs = dict(zip(plan.given, take(len(plan.given))))
    shards = dict(zip(plan.shards, take(len(plan.shards))))
    acc_in = take(1)[0] if plan.before else None
    kron_ref = take(1)[0] if plan.last else None
    w_refs.update(zip(plan.made, take(len(plan.made))))
    if plan.prepare_last:
        spread_site(terms, rights, phys, packs, [(3, k) for k in range(plan.packs)], take(1)[0])
    targets = take(4 if plan.last else 1)
    y_ref = take(1)[0]
    if not plan.last:
        kron_ref = take(1)[0]
        spread_site(terms, rights, phys, packs, plan.chunks, kron_ref)
    alive = [live_ref[0, terms * (1 + rights) + b] for b in range(rights)]
    for k in plan.made:
        right_matrices(terms, rights, numbers[k], alive, packs[k], w_refs[k])
    for n, (q, k) in enumerate(plan.chunks):
        turn_shard(terms, numbers[k], packs[k], w_refs[k], shards[q], y_ref, n * terms * SUB)
    for i in range(y_ref.shape[0]):
        total = matmul(kron_ref[...], y_ref[i])
        if plan.before:
            total = total + acc_in[i]
        if not plan.last:
            targets[0][i] = total
            continue
        width = total.shape[1]
        count = total.shape[0] // SUB // 4
        for n, target in enumerate(targets):
            for m in range(count):
                start = (n * count + m) * SUB
                target[i * SUB : (i + 1) * SUB, m * width : (m + 1) * width] = total[
                    start : start + SUB, :
                ].astype(target.dtype)


def in_hbm(x):
    return pltpu.with_memory_space_constraint(x, pltpu.HBM)


def call(body, out_shape, in_specs, scratch=(), out_specs=None, name=None, vmem=VMEM_BYTES, flops=1000):
    extra = {} if out_specs is None else {"out_specs": out_specs}
    return pl.pallas_call(
        body,
        out_shape=out_shape,
        in_specs=in_specs,
        scratch_shapes=scratch,
        compiler_params=pltpu.CompilerParams(vmem_limit_bytes=vmem),
        cost_estimate=pl.CostEstimate(flops=flops, bytes_accessed=1000, transcendentals=0),
        name=name,
        **extra,
    )


def by_states(
    wavefunction, left_blocks, right_blocks, site_terms, left_source, right_source, live_pairs
):
    all_rows = wavefunction.shape[0]
    terms, _, block, _ = left_blocks.shape
    rights = right_blocks.shape[1]
    phys = site_terms.shape[1]
    width = rights * block
    slots = 4
    rows = phys * SUB
    tiles = block // SUB
    smem = pl.BlockSpec(memory_space=pltpu.SMEM)
    vmem = pl.BlockSpec(memory_space=pltpu.VMEM)
    hbm = pl.BlockSpec(memory_space=pltpu.HBM)

    pack_rows = terms * (1 + rights) * block + phys + SUB
    mine = call(
        slice_body,
        jax.ShapeDtypeStruct((all_rows, width), BF16),
        [hbm],
        [pltpu.SemaphoreType.DMA],
        out_specs=vmem,
        name="own_states",
        vmem=SLICE_BYTES,
    )(in_hbm(wavefunction))

    def swap(x):
        return lax.ppermute(x, "mpo", CORE)

    pack = call(
        functools.partial(pack_body, terms, rights, phys),
        jax.ShapeDtypeStruct((pack_rows, block), BF16),
        [hbm] * 6,
        [
            pltpu.VMEM(right_blocks.shape, BF16),
            pltpu.VMEM(site_terms.shape, BF16),
            pltpu.SMEM(left_source.shape, jnp.int32),
            pltpu.SMEM(right_source.T.shape, jnp.int32),
            pltpu.SMEM(live_pairs.T.shape, jnp.int32),
            pltpu.SemaphoreType.DMA((terms + 5,)),
        ],
        out_specs=vmem,
        name="pack_operators",
        vmem=PACK_BYTES,
    )(
        *[
            in_hbm(x)
            for x in (
                left_blocks, right_blocks, site_terms, left_source, right_source.T, live_pairs.T
            )
        ]
    )

    def numbers_of(p):
        return p[pack_rows - SUB : pack_rows - SUB + 1, :].astype(jnp.int32)

    one_pack = terms * SUB
    quarter = (block, phys // slots * width)

    def run(name, plan, packs, numbers, shards, acc=None, w=(), kron=None, flops=1000):
        depth = len(plan.chunks) * one_pack
        shapes = [jax.ShapeDtypeStruct((terms, width, width), BF16) for _ in plan.made]
        if plan.prepare_last:
            shapes.append(jax.ShapeDtypeStruct((rows, len(packs) * one_pack), BF16))
        if plan.last:
            shapes += [jax.ShapeDtypeStruct(quarter, t) for t in (BF16, BF16, F32, F32)]
        else:
            shapes.append(jax.ShapeDtypeStruct((tiles, rows, width), F32))
        arrays = [*packs, *w, *shards] + [a for a in (acc, kron) if a is not None]
        scratch = [pltpu.VMEM((tiles, depth, width), BF16)]
        if not plan.last:
            scratch.append(pltpu.VMEM((rows, depth), BF16))
        return call(
            functools.partial(terms_body, terms, rights, phys, plan),
            tuple(shapes),
            [smem] * (1 + len(numbers)) + [vmem] * len(arrays),
            scratch,
            name=name,
            flops=flops,
        )(numbers[0], *numbers, *arrays)

    far = lax.ppermute(mine, "blk", FAR)
    near = lax.ppermute(mine, "blk", NEAR)
    pack_x = lax.ppermute(pack, "mpo", ACROSS)
    number = numbers_of(pack)
    w_own, acc = run(
        "own_pack_own_shard",
        Plan(1, [(0, 0)], made=(0,), before=False),
        (pack,),
        (number,),
        (mine,),
        flops=OWN_FLOPS,
    )
    far, acc, pack, mine = lax.optimization_barrier((far, acc, pack, mine))
    farthest = lax.ppermute(far, "blk", NEAR)
    pack_c = swap(pack)
    (acc,) = run(
        "own_pack_near_far",
        Plan(1, [(1, 0), (2, 0)]),
        (pack,),
        (number,),
        (near, far),
        acc,
        (w_own,),
        flops=CHIP_FLOPS,
    )
    acc, pack_x, pack_c = lax.optimization_barrier((acc, pack_x, pack_c))
    number_c = numbers_of(pack_c)
    x_packs = (pack_x, swap(pack_x))
    x_numbers = [numbers_of(p) for p in x_packs]
    w_core, acc = run(
        "core_pack",
        Plan(1, [(0, 0), (1, 0), (2, 0)], made=(0,)),
        (pack_c,),
        (number_c,),
        (mine, near, far),
        acc,
        flops=CORE_FLOPS,
    )
    packs, numbers = (pack, pack_c, *x_packs), (number, number_c, *x_numbers)
    w_x, w_xc, kron, acc = run(
        "other_packs",
        Plan(4, [(q, k) for q in (0, 1, 2) for k in (2, 3)], made=(2, 3), prepare_last=True),
        packs,
        numbers,
        (mine, near, far),
        acc,
        flops=OTHER_FLOPS,
    )
    farthest, acc = lax.optimization_barrier((farthest, acc))
    give_far, give_core, keep_x, keep = run(
        "third_shard",
        Plan(4, [(3, k) for k in range(4)], last=True),
        packs,
        numbers,
        (farthest,),
        acc,
        (w_own, w_core, w_x, w_xc),
        kron,
    )
    give = (keep_x + swap(give_far).astype(F32)).astype(BF16)
    taken = lax.ppermute(give, "mpo", ACROSS)
    return (keep + swap(give_core).astype(F32) + taken.astype(F32)).astype(BF16)


def solution(mesh):
    sizes = dict(mesh.shape)

    def on_device(
        wavefunction, left_blocks, right_blocks, site_terms, left_source, right_source, live_pairs
    ):
        columns = wavefunction.shape[1]
        terms, sectors, block, _ = left_blocks.shape
        phys, rights = site_terms.shape[1], right_blocks.shape[1]
        square = sizes["blk"] == 4 and sizes["mpo"] == 4 and sectors == 1 and rights == 2
        fits = columns == 4 * rights * block and phys == 16 and block == 128 and terms == 4
        step = by_states if square and fits else by_terms
        return step(
            wavefunction, left_blocks, right_blocks, site_terms, left_source, right_source, live_pairs
        )

    return jax.shard_map(
        on_device,
        mesh=mesh,
        in_specs=(
            P("rep", "blk"),
            P(("rep", "mpo"), "blk", None, None),
            P(("rep", "mpo"), None, None, None),
            P(("rep", "mpo"), None, None),
            P(("rep", "mpo"), None),
            P(("rep", "mpo"), None),
            P("rep", None),
        ),
        out_specs=P(("rep", "blk"), "mpo"),
        check_vma=False,
    )
```

```python
import functools

import jax
import jax.numpy as jnp
from jax import lax
from jax.experimental import pallas as pl
from jax.experimental.pallas import tpu as pltpu
from jax.sharding import PartitionSpec as P

F32 = jnp.float32
BF16 = jnp.bfloat16
VMEM_BYTES = 32 * 1024 * 1024
SLICE_BYTES = 32 * 1024 * 1024
PACK_BYTES = 32 * 1024 * 1024
OWN_FLOPS = 1000
CHIP_FLOPS = int(8e9)
OTHER_FLOPS = 1000
CORE_FLOPS = int(3e9)
NEAR = ((0, 1), (1, 0), (2, 3), (3, 2))
FAR = ((0, 2), (2, 0), (1, 3), (3, 1))
CORE = ((0, 1), (1, 0), (2, 3), (3, 2))
ACROSS = ((0, 2), (2, 0), (1, 3), (3, 1))
SUB = 16


def carry_left(blocks, sources, pieces):
    picked = jnp.take(blocks, sources, axis=0)
    return jnp.einsum(
        "...aij,...ajc->...aic", pieces, picked, preferred_element_type=F32
    ).astype(BF16)


def apply_right(received, site_one, source_one, right_one, physical, right_count, block_rows):
    shaped = received.reshape(received.shape[0], physical, right_count, block_rows)
    turned = jnp.einsum(
        "st,itrj->isrj", site_one, shaped, preferred_element_type=F32
    ).astype(BF16)
    picked = jnp.take(turned, source_one, axis=2)
    return jnp.einsum("isbj,bkj->isbk", picked, right_one, preferred_element_type=F32)


def by_terms(
    wavefunction, left_blocks, right_blocks, site_terms, left_source, right_source, live_pairs
):
    all_rows, columns = wavefunction.shape
    term_count, own_sectors, block_rows = left_blocks.shape[:3]
    physical = site_terms.shape[1]
    right_count = right_blocks.shape[1]
    own_rows = own_sectors * block_rows
    blocks = wavefunction.reshape(all_rows // block_rows, block_rows, columns)
    accumulated = jnp.zeros((own_rows, physical, right_count, block_rows), F32)
    for member in range(term_count):
        pieces = lax.all_gather(left_blocks[member], "blk", axis=0, tiled=True)
        carried = carry_left(blocks, left_source[member], pieces)
        received = lax.all_to_all(
            carried.reshape(all_rows, columns), "blk", split_axis=0, concat_axis=1, tiled=True
        )
        accumulated = accumulated + apply_right(
            received,
            site_terms[member],
            right_source[member],
            right_blocks[member],
            physical,
            right_count,
            block_rows,
        )
    position = lax.axis_index("blk")
    live_rows = lax.dynamic_slice_in_dim(live_pairs, position * own_sectors, own_sectors, 0)
    row_mask = jnp.repeat(live_rows.astype(F32), block_rows, axis=0)
    accumulated = accumulated * row_mask[:, None, :, None]
    flattened = accumulated.reshape(own_rows, physical * right_count * block_rows)
    summed = lax.psum_scatter(flattened, "mpo", scatter_dimension=1, tiled=True)
    return summed.astype(BF16)


def matmul(a, b):
    return jnp.dot(a, b, preferred_element_type=F32)


def slice_body(wave_ref, own_ref, sem):
    width = own_ref.shape[1]
    start = pl.multiple_of(lax.axis_index("mpo") * width, width)
    copy = pltpu.make_async_copy(wave_ref.at[:, pl.ds(start, width)], own_ref, sem)
    copy.start()
    copy.wait()


def pack_body(
    terms, rights, phys, left_hbm, right_hbm, site_hbm, sources_hbm, rsource_hbm, live_hbm,
    pack_ref, right_ref, site_ref, sources_ref, rsource_ref, live_ref, sems,
):
    block = right_ref.shape[-1]
    own_blk = lax.axis_index("blk")
    inputs = [
        (right_hbm, right_ref),
        (site_hbm, site_ref),
        (sources_hbm, sources_ref),
        (rsource_hbm, rsource_ref),
        (live_hbm, live_ref),
    ]
    for w in range(terms):
        inputs.append((left_hbm.at[w, 0], pack_ref.at[pl.ds(w * block, block), :]))
    copies = [
        pltpu.make_async_copy(source, target, sems.at[n])
        for n, (source, target) in enumerate(inputs)
    ]
    for copy in copies:
        copy.start()
    for copy in copies[1:5]:
        copy.wait()
    base = terms * (1 + rights) * block
    lane = lax.broadcasted_iota(jnp.int32, (phys, block), 1)
    row = lax.broadcasted_iota(jnp.int32, (phys, block), 0)
    site = jnp.zeros((phys, block), F32)
    for w in range(terms):
        spot = jnp.where(lane == row + w * phys, 1.0, 0.0).astype(BF16)
        site = site + matmul(site_ref[w], spot)
    pack_ref[base : base + phys, :] = site.astype(BF16)
    numbers = jnp.zeros((SUB, block), F32)
    lane = lax.broadcasted_iota(jnp.int32, (SUB, block), 1)
    for w in range(terms):
        numbers = jnp.where(lane == w, sources_ref[w, own_blk].astype(F32), numbers)
        for b in range(rights):
            at = terms + w * rights + b
            numbers = jnp.where(lane == at, rsource_ref[b, w].astype(F32), numbers)
    for b in range(rights):
        at = terms * (1 + rights) + b
        numbers = jnp.where(lane == at, live_ref[b, own_blk].astype(F32), numbers)
    pack_ref[base + phys : base + phys + SUB, :] = numbers.astype(BF16)
    copies[0].wait()
    for w in range(terms):
        for b in range(rights):
            at = (terms + w * rights + b) * block
            pack_ref[at : at + block, :] = right_ref[w, b].astype(F32).T.astype(BF16)
    for copy in copies[5:]:
        copy.wait()


def right_matrices(terms, rights, numbers, alive, pack, w_ref):
    block = pack.shape[-1]
    for w in range(terms):
        for b in range(rights):
            start = (terms + w * rights + b) * block
            turned = pack[start : start + block, :]
            source = numbers[0, terms + w * rights + b]
            for r in range(rights):
                keep = jnp.logical_and(source == r, alive[b] != 0)
                w_ref[w, r * block : (r + 1) * block, b * block : (b + 1) * block] = jnp.where(
                    keep, turned, jnp.zeros_like(turned)
                )


def spread_site(terms, rights, phys, packs, chunks, kron_ref):
    block = packs[0].shape[-1]
    me, own_blk = lax.axis_index("mpo"), lax.axis_index("blk")
    site_at = (1 + rights) * terms * block
    site = jnp.concatenate([p[site_at : site_at + phys, :] for p in packs], axis=1)
    rows, depth = kron_ref.shape
    quarter, here = phys // 4, len(packs) * block
    srow = lax.broadcasted_iota(jnp.int32, (rows, phys), 0) >> 4
    turn = srow >> 2
    owner = lax.bitwise_xor(me, jnp.where(turn == 0, 3, jnp.where(turn == 3, 0, turn)))
    swant = owner * quarter + (srow & 3)
    pick_s = jnp.where(
        lax.broadcasted_iota(jnp.int32, (rows, phys), 1) == swant, 1.0, 0.0
    ).astype(BF16)
    slot = lax.broadcasted_iota(jnp.int32, (1, depth), 1) >> 4
    want = jnp.zeros((1, depth), jnp.int32)
    for n, (shard, pack) in enumerate(chunks):
        state = lax.bitwise_xor(own_blk, shard) * quarter + me
        spot = pack * block + (slot - n * terms) * phys + state
        want = jnp.where(jnp.logical_and(slot >= n * terms, slot < (n + 1) * terms), spot, want)
    pick_t = jnp.where(
        lax.broadcasted_iota(jnp.int32, (here, depth), 0) == want, 1.0, 0.0
    ).astype(BF16)
    spread = matmul(pick_s, matmul(site, pick_t).astype(BF16))
    diagonal = (lax.broadcasted_iota(jnp.int32, (rows, depth), 0) & 15) == (
        lax.broadcasted_iota(jnp.int32, (rows, depth), 1) & 15
    )
    kron_ref[...] = jnp.where(diagonal, spread, 0.0).astype(BF16)


def left_products(terms, numbers, pack, shards, c_ref, starts):
    block = pack.shape[-1]
    for w in range(terms):
        row = pl.multiple_of(numbers[0, w] * block, block)
        left = pack[w * block : (w + 1) * block, :]
        for start, shard in zip(starts, shards):
            c_ref[start + w] = matmul(left, shard[pl.ds(row, block), :]).astype(BF16)


def right_products(terms, w_ref, c_ref, y_ref, starts):
    tiles = y_ref.shape[0]
    for w in range(terms):
        for start in starts:
            y = matmul(c_ref[start + w], w_ref[w]).astype(BF16)
            at = (start + w) * SUB
            y_ref[:, at : at + SUB, :] = y.reshape(tiles, SUB, y.shape[-1])


class Plan:
    def __init__(self, packs, chunks, made=(), before=True, prepare_last=False, last=False):
        self.packs, self.chunks, self.made = packs, chunks, made
        self.before, self.prepare_last, self.last = before, prepare_last, last
        self.used = sorted({k for _, k in chunks})
        self.given = [k for k in self.used if k not in made]
        self.shards = sorted({q for q, _ in chunks})


def terms_body(terms, rights, phys, plan, live_ref, *refs):
    refs = list(refs)

    def take(count):
        taken, refs[:] = refs[:count], refs[count:]
        return taken

    numbers, packs = take(plan.packs), take(plan.packs)
    w_refs = dict(zip(plan.given, take(len(plan.given))))
    shards = dict(zip(plan.shards, take(len(plan.shards))))
    acc_in = take(1)[0] if plan.before else None
    kron_ref = take(1)[0] if plan.last else None
    w_refs.update(zip(plan.made, take(len(plan.made))))
    if plan.prepare_last:
        spread_site(terms, rights, phys, packs, [(3, k) for k in range(plan.packs)], take(1)[0])
    targets = take(4 if plan.last else 1)
    c_ref, y_ref = take(2)
    if not plan.last:
        kron_ref = take(1)[0]
        spread_site(terms, rights, phys, packs, plan.chunks, kron_ref)
    alive = [live_ref[0, terms * (1 + rights) + b] for b in range(rights)]
    for k in plan.made:
        right_matrices(terms, rights, numbers[k], alive, packs[k], w_refs[k])
    starts = {k: [n * terms for n, (_, pack) in enumerate(plan.chunks) if pack == k] for k in plan.used}
    for k in plan.used:
        sources = [shards[q] for q, pack in plan.chunks if pack == k]
        left_products(terms, numbers[k], packs[k], sources, c_ref, starts[k])
    for k in plan.used:
        right_products(terms, w_refs[k], c_ref, y_ref, starts[k])
    for i in range(y_ref.shape[0]):
        total = matmul(kron_ref[...], y_ref[i])
        if plan.before:
            total = total + acc_in[i]
        if not plan.last:
            targets[0][i] = total
            continue
        width = total.shape[1]
        count = total.shape[0] // SUB // 4
        for n, target in enumerate(targets):
            for m in range(count):
                start = (n * count + m) * SUB
                target[i * SUB : (i + 1) * SUB, m * width : (m + 1) * width] = total[
                    start : start + SUB, :
                ].astype(target.dtype)


def in_hbm(x):
    return pltpu.with_memory_space_constraint(x, pltpu.HBM)


def call(body, out_shape, in_specs, scratch=(), out_specs=None, name=None, vmem=VMEM_BYTES, flops=1000):
    extra = {} if out_specs is None else {"out_specs": out_specs}
    return pl.pallas_call(
        body,
        out_shape=out_shape,
        in_specs=in_specs,
        scratch_shapes=scratch,
        compiler_params=pltpu.CompilerParams(vmem_limit_bytes=vmem),
        cost_estimate=pl.CostEstimate(flops=flops, bytes_accessed=1000, transcendentals=0),
        name=name,
        **extra,
    )


def by_states(
    wavefunction, left_blocks, right_blocks, site_terms, left_source, right_source, live_pairs
):
    all_rows = wavefunction.shape[0]
    terms, _, block, _ = left_blocks.shape
    rights = right_blocks.shape[1]
    phys = site_terms.shape[1]
    width = rights * block
    slots = 4
    rows = phys * SUB
    tiles = block // SUB
    smem = pl.BlockSpec(memory_space=pltpu.SMEM)
    vmem = pl.BlockSpec(memory_space=pltpu.VMEM)
    hbm = pl.BlockSpec(memory_space=pltpu.HBM)

    pack_rows = terms * (1 + rights) * block + phys + SUB
    mine = call(
        slice_body,
        jax.ShapeDtypeStruct((all_rows, width), BF16),
        [hbm],
        [pltpu.SemaphoreType.DMA],
        out_specs=vmem,
        name="own_states",
        vmem=SLICE_BYTES,
    )(in_hbm(wavefunction))

    def swap(x):
        return lax.ppermute(x, "mpo", CORE)

    pack = call(
        functools.partial(pack_body, terms, rights, phys),
        jax.ShapeDtypeStruct((pack_rows, block), BF16),
        [hbm] * 6,
        [
            pltpu.VMEM(right_blocks.shape, BF16),
            pltpu.VMEM(site_terms.shape, BF16),
            pltpu.SMEM(left_source.shape, jnp.int32),
            pltpu.SMEM(right_source.T.shape, jnp.int32),
            pltpu.SMEM(live_pairs.T.shape, jnp.int32),
            pltpu.SemaphoreType.DMA((terms + 5,)),
        ],
        out_specs=vmem,
        name="pack_operators",
        vmem=PACK_BYTES,
    )(
        *[
            in_hbm(x)
            for x in (
                left_blocks, right_blocks, site_terms, left_source, right_source.T, live_pairs.T
            )
        ]
    )

    def numbers_of(p):
        return p[pack_rows - SUB : pack_rows - SUB + 1, :].astype(jnp.int32)

    one_pack = terms * SUB
    quarter = (block, phys // slots * width)

    def run(name, plan, packs, numbers, shards, acc=None, w=(), kron=None, flops=1000):
        depth = len(plan.chunks) * one_pack
        shapes = [jax.ShapeDtypeStruct((terms, width, width), BF16) for _ in plan.made]
        if plan.prepare_last:
            shapes.append(jax.ShapeDtypeStruct((rows, len(packs) * one_pack), BF16))
        if plan.last:
            shapes += [jax.ShapeDtypeStruct(quarter, t) for t in (BF16, BF16, F32, F32)]
        else:
            shapes.append(jax.ShapeDtypeStruct((tiles, rows, width), F32))
        arrays = [*packs, *w, *shards] + [a for a in (acc, kron) if a is not None]
        scratch = [
            pltpu.VMEM((len(plan.chunks) * terms, block, width), BF16),
            pltpu.VMEM((tiles, depth, width), BF16),
        ]
        if not plan.last:
            scratch.append(pltpu.VMEM((rows, depth), BF16))
        return call(
            functools.partial(terms_body, terms, rights, phys, plan),
            tuple(shapes),
            [smem] * (1 + len(numbers)) + [vmem] * len(arrays),
            scratch,
            name=name,
            flops=flops,
        )(numbers[0], *numbers, *arrays)

    far = lax.ppermute(mine, "blk", FAR)
    near = lax.ppermute(mine, "blk", NEAR)
    pack_x = lax.ppermute(pack, "mpo", ACROSS)
    number = numbers_of(pack)
    w_own, acc = run(
        "own_pack_own_shard",
        Plan(1, [(0, 0)], made=(0,), before=False),
        (pack,),
        (number,),
        (mine,),
        flops=OWN_FLOPS,
    )
    pack_c = swap(pack)
    far, acc, mine = lax.optimization_barrier((far, acc, mine))
    farthest = lax.ppermute(far, "blk", NEAR)
    (acc,) = run(
        "own_pack_near_far",
        Plan(1, [(1, 0), (2, 0)]),
        (pack,),
        (number,),
        (near, far),
        acc,
        (w_own,),
        flops=CHIP_FLOPS,
    )
    acc, pack_x, pack_c = lax.optimization_barrier((acc, pack_x, pack_c))
    number_c = numbers_of(pack_c)
    x_packs = (pack_x, swap(pack_x))
    x_numbers = [numbers_of(p) for p in x_packs]
    w_core, acc = run(
        "core_pack",
        Plan(1, [(0, 0), (1, 0), (2, 0)], made=(0,)),
        (pack_c,),
        (number_c,),
        (mine, near, far),
        acc,
        flops=CORE_FLOPS,
    )
    packs, numbers = (pack, pack_c, *x_packs), (number, number_c, *x_numbers)
    w_x, w_xc, kron, acc = run(
        "other_packs",
        Plan(4, [(q, k) for q in (0, 1, 2) for k in (2, 3)], made=(2, 3), prepare_last=True),
        packs,
        numbers,
        (mine, near, far),
        acc,
        flops=OTHER_FLOPS,
    )
    farthest, acc = lax.optimization_barrier((farthest, acc))
    give_far, give_core, keep_x, keep = run(
        "third_shard",
        Plan(4, [(3, k) for k in range(4)], last=True),
        packs,
        numbers,
        (farthest,),
        acc,
        (w_own, w_core, w_x, w_xc),
        kron,
    )
    give = (keep_x + swap(give_far).astype(F32)).astype(BF16)
    taken = lax.ppermute(give, "mpo", ACROSS)
    return (keep + swap(give_core).astype(F32) + taken.astype(F32)).astype(BF16)


def solution(mesh):
    sizes = dict(mesh.shape)

    def on_device(
        wavefunction, left_blocks, right_blocks, site_terms, left_source, right_source, live_pairs
    ):
        columns = wavefunction.shape[1]
        terms, sectors, block, _ = left_blocks.shape
        phys, rights = site_terms.shape[1], right_blocks.shape[1]
        square = sizes["blk"] == 4 and sizes["mpo"] == 4 and sectors == 1 and rights == 2
        fits = columns == 4 * rights * block and phys == 16 and block == 128 and terms == 4
        step = by_states if square and fits else by_terms
        return step(
            wavefunction, left_blocks, right_blocks, site_terms, left_source, right_source, live_pairs
        )

    return jax.shard_map(
        on_device,
        mesh=mesh,
        in_specs=(
            P("rep", "blk"),
            P(("rep", "mpo"), "blk", None, None),
            P(("rep", "mpo"), None, None, None),
            P(("rep", "mpo"), None, None),
            P(("rep", "mpo"), None),
            P(("rep", "mpo"), None),
            P("rep", None),
        ),
        out_specs=P(("rep", "blk"), "mpo"),
        check_vma=False,
    )
```

```python
import functools

import jax
import jax.numpy as jnp
from jax import lax
from jax.experimental import pallas as pl
from jax.experimental.pallas import tpu as pltpu
from jax.sharding import PartitionSpec as P

F32 = jnp.float32
BF16 = jnp.bfloat16
VMEM_BYTES = 32 * 1024 * 1024
SLICE_BYTES = 32 * 1024 * 1024
PACK_BYTES = 32 * 1024 * 1024
OWN_FLOPS = 1000
CHIP_FLOPS = int(8e9)
CORE_FLOPS = int(3e9)
NEAR = ((0, 1), (1, 0), (2, 3), (3, 2))
FAR = ((0, 2), (2, 0), (1, 3), (3, 1))
CORE = ((0, 1), (1, 0), (2, 3), (3, 2))
ACROSS = ((0, 2), (2, 0), (1, 3), (3, 1))
PARTS = 2
SUB = 16


def carry_left(blocks, sources, pieces):
    picked = jnp.take(blocks, sources, axis=0)
    return jnp.einsum(
        "...aij,...ajc->...aic", pieces, picked, preferred_element_type=F32
    ).astype(BF16)


def apply_right(received, site_one, source_one, right_one, physical, right_count, block_rows):
    shaped = received.reshape(received.shape[0], physical, right_count, block_rows)
    turned = jnp.einsum(
        "st,itrj->isrj", site_one, shaped, preferred_element_type=F32
    ).astype(BF16)
    picked = jnp.take(turned, source_one, axis=2)
    return jnp.einsum("isbj,bkj->isbk", picked, right_one, preferred_element_type=F32)


def by_terms(
    wavefunction, left_blocks, right_blocks, site_terms, left_source, right_source, live_pairs
):
    all_rows, columns = wavefunction.shape
    term_count, own_sectors, block_rows = left_blocks.shape[:3]
    physical = site_terms.shape[1]
    right_count = right_blocks.shape[1]
    own_rows = own_sectors * block_rows
    blocks = wavefunction.reshape(all_rows // block_rows, block_rows, columns)
    accumulated = jnp.zeros((own_rows, physical, right_count, block_rows), F32)
    for member in range(term_count):
        pieces = lax.all_gather(left_blocks[member], "blk", axis=0, tiled=True)
        carried = carry_left(blocks, left_source[member], pieces)
        received = lax.all_to_all(
            carried.reshape(all_rows, columns), "blk", split_axis=0, concat_axis=1, tiled=True
        )
        accumulated = accumulated + apply_right(
            received,
            site_terms[member],
            right_source[member],
            right_blocks[member],
            physical,
            right_count,
            block_rows,
        )
    position = lax.axis_index("blk")
    live_rows = lax.dynamic_slice_in_dim(live_pairs, position * own_sectors, own_sectors, 0)
    row_mask = jnp.repeat(live_rows.astype(F32), block_rows, axis=0)
    accumulated = accumulated * row_mask[:, None, :, None]
    flattened = accumulated.reshape(own_rows, physical * right_count * block_rows)
    summed = lax.psum_scatter(flattened, "mpo", scatter_dimension=1, tiled=True)
    return summed.astype(BF16)


def matmul(a, b):
    return jnp.dot(a, b, preferred_element_type=F32)


def slice_body(wave_ref, own_ref, sem):
    width = own_ref.shape[1]
    start = pl.multiple_of(lax.axis_index("mpo") * width, width)
    copy = pltpu.make_async_copy(wave_ref.at[:, pl.ds(start, width)], own_ref, sem)
    copy.start()
    copy.wait()


def pack_body(
    terms, rights, phys, left_hbm, right_hbm, site_hbm, sources_hbm, rsource_hbm, live_hbm,
    pack_ref, right_ref, site_ref, sources_ref, rsource_ref, live_ref, sems,
):
    block = right_ref.shape[-1]
    own_blk = lax.axis_index("blk")
    inputs = [
        (right_hbm, right_ref),
        (site_hbm, site_ref),
        (sources_hbm, sources_ref),
        (rsource_hbm, rsource_ref),
        (live_hbm, live_ref),
    ]
    for w in range(terms):
        inputs.append((left_hbm.at[w, 0], pack_ref.at[pl.ds(w * block, block), :]))
    copies = [
        pltpu.make_async_copy(source, target, sems.at[n])
        for n, (source, target) in enumerate(inputs)
    ]
    for copy in copies:
        copy.start()
    for copy in copies[1:5]:
        copy.wait()
    base = terms * (1 + rights) * block
    lane = lax.broadcasted_iota(jnp.int32, (phys, block), 1)
    row = lax.broadcasted_iota(jnp.int32, (phys, block), 0)
    site = jnp.zeros((phys, block), F32)
    for w in range(terms):
        spot = jnp.where(lane == row + w * phys, 1.0, 0.0).astype(BF16)
        site = site + matmul(site_ref[w], spot)
    pack_ref[base : base + phys, :] = site.astype(BF16)
    numbers = jnp.zeros((SUB, block), F32)
    lane = lax.broadcasted_iota(jnp.int32, (SUB, block), 1)
    for w in range(terms):
        numbers = jnp.where(lane == w, sources_ref[w, own_blk].astype(F32), numbers)
        for b in range(rights):
            at = terms + w * rights + b
            numbers = jnp.where(lane == at, rsource_ref[b, w].astype(F32), numbers)
    for b in range(rights):
        at = terms * (1 + rights) + b
        numbers = jnp.where(lane == at, live_ref[b, own_blk].astype(F32), numbers)
    pack_ref[base + phys : base + phys + SUB, :] = numbers.astype(BF16)
    copies[0].wait()
    for w in range(terms):
        for b in range(rights):
            at = (terms + w * rights + b) * block
            pack_ref[at : at + block, :] = right_ref[w, b].astype(F32).T.astype(BF16)
    for copy in copies[5:]:
        copy.wait()


def block_matrices(terms, rights, numbers, pack, left_ref, right_ref):
    block = pack.shape[-1]
    sectors = left_ref.shape[-1] // block
    for w in range(terms):
        left = pack[w * block : (w + 1) * block, :]
        for r in range(sectors):
            left_ref[w, :, r * block : (r + 1) * block] = jnp.where(
                numbers[0, w] == r, left, jnp.zeros_like(left)
            )
        for b in range(rights):
            start = (terms + w * rights + b) * block
            turned = pack[start : start + block, :]
            source = numbers[0, terms + w * rights + b]
            alive = numbers[0, terms * (1 + rights) + b] != 0
            for r in range(rights):
                right_ref[w, r * block : (r + 1) * block, b * block : (b + 1) * block] = jnp.where(
                    jnp.logical_and(source == r, alive), turned, jnp.zeros_like(turned)
                )


def spread_site(terms, rights, phys, packs, chunks, kron_ref):
    block = packs[0].shape[-1]
    me, own_blk = lax.axis_index("mpo"), lax.axis_index("blk")
    site_at = (1 + rights) * terms * block
    site = jnp.concatenate([p[site_at : site_at + phys, :] for p in packs], axis=1)
    rows, depth = kron_ref.shape
    quarter, here = phys // 4, len(packs) * block
    srow = lax.broadcasted_iota(jnp.int32, (rows, phys), 0) >> 4
    turn = srow >> 2
    owner = lax.bitwise_xor(me, jnp.where(turn == 0, 3, jnp.where(turn == 3, 0, turn)))
    swant = owner * quarter + (srow & 3)
    pick_s = jnp.where(
        lax.broadcasted_iota(jnp.int32, (rows, phys), 1) == swant, 1.0, 0.0
    ).astype(BF16)
    slot = lax.broadcasted_iota(jnp.int32, (1, depth), 1) >> 4
    want = jnp.zeros((1, depth), jnp.int32)
    for n, (shard, pack) in enumerate(chunks):
        state = lax.bitwise_xor(own_blk, shard) * quarter + me
        spot = pack * block + (slot - n * terms) * phys + state
        want = jnp.where(jnp.logical_and(slot >= n * terms, slot < (n + 1) * terms), spot, want)
    pick_t = jnp.where(
        lax.broadcasted_iota(jnp.int32, (here, depth), 0) == want, 1.0, 0.0
    ).astype(BF16)
    spread = matmul(pick_s, matmul(site, pick_t).astype(BF16))
    diagonal = (lax.broadcasted_iota(jnp.int32, (rows, depth), 0) & 15) == (
        lax.broadcasted_iota(jnp.int32, (rows, depth), 1) & 15
    )
    kron_ref[...] = jnp.where(diagonal, spread, 0.0).astype(BF16)


def left_products(left_ref, shards, c_ref, starts, first):
    terms, _, depth = left_ref.shape
    count = c_ref.shape[1]
    left = left_ref[:, first : first + count, :].reshape(terms * count, depth)
    for start, shard in zip(starts, shards):
        c_ref[start : start + terms] = (
            matmul(left, shard[...]).astype(BF16).reshape(terms, count, c_ref.shape[2])
        )


def right_products(terms, w_ref, c_ref, y_ref, starts):
    tiles = y_ref.shape[0]
    for w in range(terms):
        for start in starts:
            y = matmul(c_ref[start + w], w_ref[w]).astype(BF16)
            at = (start + w) * SUB
            y_ref[:, at : at + SUB, :] = y.reshape(tiles, SUB, y.shape[-1])


class Plan:
    def __init__(self, packs, chunks, made=(), before=True, prepare_last=False, last=None):
        self.packs, self.chunks, self.made = packs, chunks, made
        self.before, self.prepare_last, self.last = before, prepare_last, last
        self.used = sorted({k for _, k in chunks})
        self.given = [k for k in self.used if k not in made]
        self.shards = sorted({q for q, _ in chunks})


def terms_body(terms, rights, phys, plan, *refs):
    refs = list(refs)

    def take(count):
        taken, refs[:] = refs[:count], refs[count:]
        return taken

    last = plan.last is not None
    numbers = dict(zip(plan.made, take(len(plan.made))))
    packs = take(0 if last else plan.packs)
    lefts = dict(zip(plan.given, take(len(plan.given))))
    rights_of = dict(zip(plan.given, take(len(plan.given))))
    shards = dict(zip(plan.shards, take(len(plan.shards))))
    acc_in = take(1)[0] if plan.before else None
    kron_ref = take(1)[0] if last else None
    lefts.update(zip(plan.made, take(len(plan.made))))
    rights_of.update(zip(plan.made, take(len(plan.made))))
    if plan.prepare_last:
        spread_site(terms, rights, phys, packs, [(3, k) for k in range(plan.packs)], take(1)[0])
    targets = take(3 if last else 1)
    c_ref, y_ref = take(2)
    if not last:
        kron_ref = take(1)[0]
        spread_site(terms, rights, phys, packs, plan.chunks, kron_ref)
    for k in plan.made:
        block_matrices(terms, rights, numbers[k], packs[k], lefts[k], rights_of[k])
    starts = {k: [n * terms for n, (_, pack) in enumerate(plan.chunks) if pack == k] for k in plan.used}
    first = plan.last * c_ref.shape[1] if last else 0
    for k in plan.used:
        sources = [shards[q] for q, pack in plan.chunks if pack == k]
        left_products(lefts[k], sources, c_ref, starts[k], first)
    for k in plan.used:
        right_products(terms, rights_of[k], c_ref, y_ref, starts[k])
    for i in range(y_ref.shape[0]):
        total = matmul(kron_ref[...], y_ref[i])
        if plan.before:
            total = total + acc_in[first // SUB + i]
        if not last:
            targets[0][i] = total
            continue
        width = total.shape[1]
        count = total.shape[0] // SUB // 4
        for n, (target, place) in enumerate(
            ((targets[0], 0), (targets[0], 1), (targets[1], 0), (targets[2], 0))
        ):
            for m in range(count):
                start, column = (n * count + m) * SUB, (place * count + m) * width
                target[i * SUB : (i + 1) * SUB, column : column + width] = total[
                    start : start + SUB, :
                ].astype(target.dtype)


def in_hbm(x):
    return pltpu.with_memory_space_constraint(x, pltpu.HBM)


def call(body, out_shape, in_specs, scratch=(), out_specs=None, name=None, vmem=VMEM_BYTES, flops=1000):
    extra = {} if out_specs is None else {"out_specs": out_specs}
    return pl.pallas_call(
        body,
        out_shape=out_shape,
        in_specs=in_specs,
        scratch_shapes=scratch,
        compiler_params=pltpu.CompilerParams(vmem_limit_bytes=vmem),
        cost_estimate=pl.CostEstimate(flops=flops, bytes_accessed=1000, transcendentals=0),
        name=name,
        **extra,
    )


def by_states(
    wavefunction, left_blocks, right_blocks, site_terms, left_source, right_source, live_pairs
):
    all_rows = wavefunction.shape[0]
    terms, _, block, _ = left_blocks.shape
    rights = right_blocks.shape[1]
    phys = site_terms.shape[1]
    width = rights * block
    slots = 4
    rows = phys * SUB
    tiles = block // SUB
    smem = pl.BlockSpec(memory_space=pltpu.SMEM)
    vmem = pl.BlockSpec(memory_space=pltpu.VMEM)
    hbm = pl.BlockSpec(memory_space=pltpu.HBM)

    pack_rows = terms * (1 + rights) * block + phys + SUB
    mine = call(
        slice_body,
        jax.ShapeDtypeStruct((all_rows, width), BF16),
        [hbm],
        [pltpu.SemaphoreType.DMA],
        out_specs=vmem,
        name="own_states",
        vmem=SLICE_BYTES,
    )(in_hbm(wavefunction))

    def swap(x):
        return lax.ppermute(x, "mpo", CORE)

    pack = call(
        functools.partial(pack_body, terms, rights, phys),
        jax.ShapeDtypeStruct((pack_rows, block), BF16),
        [hbm] * 6,
        [
            pltpu.VMEM(right_blocks.shape, BF16),
            pltpu.VMEM(site_terms.shape, BF16),
            pltpu.SMEM(left_source.shape, jnp.int32),
            pltpu.SMEM(right_source.T.shape, jnp.int32),
            pltpu.SMEM(live_pairs.T.shape, jnp.int32),
            pltpu.SemaphoreType.DMA((terms + 5,)),
        ],
        out_specs=vmem,
        name="pack_operators",
        vmem=PACK_BYTES,
    )(
        *[
            in_hbm(x)
            for x in (
                left_blocks, right_blocks, site_terms, left_source, right_source.T, live_pairs.T
            )
        ]
    )

    def numbers_of(p):
        return p[pack_rows - SUB : pack_rows - SUB + 1, :].astype(jnp.int32)

    one_pack = terms * SUB

    def run(name, plan, packs, numbers, shards, acc=None, given=(), kron=None, flops=1000):
        depth = len(plan.chunks) * one_pack
        last = plan.last is not None
        part = PARTS if last else 1
        shapes = [jax.ShapeDtypeStruct((terms, block, all_rows), BF16) for _ in plan.made]
        shapes += [jax.ShapeDtypeStruct((terms, width, width), BF16) for _ in plan.made]
        if plan.prepare_last:
            shapes.append(jax.ShapeDtypeStruct((rows, len(packs) * one_pack), BF16))
        if last:
            size, columns = block // part, phys // slots * width
            shapes.append(jax.ShapeDtypeStruct((size, 2 * columns), BF16))
            shapes += [jax.ShapeDtypeStruct((size, columns), F32)] * 2
        else:
            shapes.append(jax.ShapeDtypeStruct((tiles, rows, width), F32))
        lefts, rights_of = [g[0] for g in given], [g[1] for g in given]
        arrays = [*packs, *lefts, *rights_of, *shards]
        arrays += [a for a in (acc, kron) if a is not None]
        scratch = [
            pltpu.VMEM((len(plan.chunks) * terms, block // part, width), BF16),
            pltpu.VMEM((tiles // part, depth, width), BF16),
        ]
        if not last:
            scratch.append(pltpu.VMEM((rows, depth), BF16))
        outs = call(
            functools.partial(terms_body, terms, rights, phys, plan),
            tuple(shapes),
            [smem] * len(numbers) + [vmem] * len(arrays),
            scratch,
            name=name,
            flops=flops,
        )(*numbers, *arrays)
        made = len(plan.made)
        return tuple(zip(outs[:made], outs[made : 2 * made])) + tuple(outs[2 * made :])

    far = lax.ppermute(mine, "blk", FAR)
    near = lax.ppermute(mine, "blk", NEAR)
    pack_x = lax.ppermute(pack, "mpo", ACROSS)
    own, acc = run(
        "own_pack_own_shard",
        Plan(1, [(0, 0)], made=(0,), before=False),
        (pack,),
        (numbers_of(pack),),
        (mine,),
        flops=OWN_FLOPS,
    )
    pack_c = swap(pack)
    far, acc, mine = lax.optimization_barrier((far, acc, mine))
    farthest = lax.ppermute(far, "blk", NEAR)
    (acc,) = run(
        "own_pack_near_far",
        Plan(1, [(1, 0), (2, 0)]),
        (pack,),
        (),
        (near, far),
        acc,
        (own,),
        flops=CHIP_FLOPS,
    )
    acc, pack_x, pack_c = lax.optimization_barrier((acc, pack_x, pack_c))
    x_packs = (pack_x, swap(pack_x))
    core, acc = run(
        "core_pack",
        Plan(1, [(0, 0), (1, 0), (2, 0)], made=(0,)),
        (pack_c,),
        (numbers_of(pack_c),),
        (mine, near, far),
        acc,
        flops=CORE_FLOPS,
    )
    across, beyond, kron, acc = run(
        "other_packs",
        Plan(4, [(q, k) for q in (0, 1, 2) for k in (2, 3)], made=(2, 3), prepare_last=True),
        (pack, pack_c, *x_packs),
        [numbers_of(p) for p in x_packs],
        (mine, near, far),
        acc,
    )
    farthest, acc = lax.optimization_barrier((farthest, acc))
    outs = []
    for part in range(PARTS):
        give, keep_x, keep = run(
            "third_shard",
            Plan(4, [(3, k) for k in range(4)], last=part),
            (),
            (),
            (farthest,),
            acc,
            (own, core, across, beyond),
            kron,
        )
        columns = keep.shape[1]
        back = swap(give)
        send = (keep_x + back[:, :columns].astype(F32)).astype(BF16)
        taken = lax.ppermute(send, "mpo", ACROSS)
        outs.append((keep + back[:, columns:].astype(F32) + taken.astype(F32)).astype(BF16))
    return jnp.concatenate(outs, axis=0) if PARTS > 1 else outs[0]


def solution(mesh):
    sizes = dict(mesh.shape)

    def on_device(
        wavefunction, left_blocks, right_blocks, site_terms, left_source, right_source, live_pairs
    ):
        columns = wavefunction.shape[1]
        terms, sectors, block, _ = left_blocks.shape
        phys, rights = site_terms.shape[1], right_blocks.shape[1]
        square = sizes["blk"] == 4 and sizes["mpo"] == 4 and sectors == 1 and rights == 2
        fits = columns == 4 * rights * block and phys == 16 and block == 128 and terms == 4
        step = by_states if square and fits else by_terms
        return step(
            wavefunction, left_blocks, right_blocks, site_terms, left_source, right_source, live_pairs
        )

    return jax.shard_map(
        on_device,
        mesh=mesh,
        in_specs=(
            P("rep", "blk"),
            P(("rep", "mpo"), "blk", None, None),
            P(("rep", "mpo"), None, None, None),
            P(("rep", "mpo"), None, None),
            P(("rep", "mpo"), None),
            P(("rep", "mpo"), None),
            P("rep", None),
        ),
        out_specs=P(("rep", "blk"), "mpo"),
        check_vma=False,
    )
```

```python
import functools

import jax
import jax.numpy as jnp
from jax import lax
from jax.experimental import pallas as pl
from jax.experimental.pallas import tpu as pltpu
from jax.sharding import PartitionSpec as P

F32 = jnp.float32
BF16 = jnp.bfloat16
VMEM_BYTES = 32 * 1024 * 1024
SLICE_BYTES = 32 * 1024 * 1024
PACK_BYTES = 32 * 1024 * 1024
OWN_FLOPS = 1000
CHIP_FLOPS = int(8e9)
CORE_FLOPS = int(3e9)
NEAR = ((0, 1), (1, 0), (2, 3), (3, 2))
FAR = ((0, 2), (2, 0), (1, 3), (3, 1))
CORE = ((0, 1), (1, 0), (2, 3), (3, 2))
ACROSS = ((0, 2), (2, 0), (1, 3), (3, 1))
PARTS = 2
SUB = 16


def carry_left(blocks, sources, pieces):
    picked = jnp.take(blocks, sources, axis=0)
    return jnp.einsum(
        "...aij,...ajc->...aic", pieces, picked, preferred_element_type=F32
    ).astype(BF16)


def apply_right(received, site_one, source_one, right_one, physical, right_count, block_rows):
    shaped = received.reshape(received.shape[0], physical, right_count, block_rows)
    turned = jnp.einsum(
        "st,itrj->isrj", site_one, shaped, preferred_element_type=F32
    ).astype(BF16)
    picked = jnp.take(turned, source_one, axis=2)
    return jnp.einsum("isbj,bkj->isbk", picked, right_one, preferred_element_type=F32)


def by_terms(
    wavefunction, left_blocks, right_blocks, site_terms, left_source, right_source, live_pairs
):
    all_rows, columns = wavefunction.shape
    term_count, own_sectors, block_rows = left_blocks.shape[:3]
    physical = site_terms.shape[1]
    right_count = right_blocks.shape[1]
    own_rows = own_sectors * block_rows
    blocks = wavefunction.reshape(all_rows // block_rows, block_rows, columns)
    accumulated = jnp.zeros((own_rows, physical, right_count, block_rows), F32)
    for member in range(term_count):
        pieces = lax.all_gather(left_blocks[member], "blk", axis=0, tiled=True)
        carried = carry_left(blocks, left_source[member], pieces)
        received = lax.all_to_all(
            carried.reshape(all_rows, columns), "blk", split_axis=0, concat_axis=1, tiled=True
        )
        accumulated = accumulated + apply_right(
            received,
            site_terms[member],
            right_source[member],
            right_blocks[member],
            physical,
            right_count,
            block_rows,
        )
    position = lax.axis_index("blk")
    live_rows = lax.dynamic_slice_in_dim(live_pairs, position * own_sectors, own_sectors, 0)
    row_mask = jnp.repeat(live_rows.astype(F32), block_rows, axis=0)
    accumulated = accumulated * row_mask[:, None, :, None]
    flattened = accumulated.reshape(own_rows, physical * right_count * block_rows)
    summed = lax.psum_scatter(flattened, "mpo", scatter_dimension=1, tiled=True)
    return summed.astype(BF16)


def matmul(a, b):
    return jnp.dot(a, b, preferred_element_type=F32)


def slice_body(wave_ref, own_ref, sem):
    width = own_ref.shape[1]
    start = pl.multiple_of(lax.axis_index("mpo") * width, width)
    copy = pltpu.make_async_copy(wave_ref.at[:, pl.ds(start, width)], own_ref, sem)
    copy.start()
    copy.wait()


def pack_body(
    terms, rights, phys, left_hbm, right_hbm, site_hbm, sources_hbm, rsource_hbm, live_hbm,
    pack_ref, right_ref, site_ref, sources_ref, rsource_ref, live_ref, sems,
):
    block = right_ref.shape[-1]
    own_blk = lax.axis_index("blk")
    inputs = [
        (right_hbm, right_ref),
        (site_hbm, site_ref),
        (sources_hbm, sources_ref),
        (rsource_hbm, rsource_ref),
        (live_hbm, live_ref),
    ]
    for w in range(terms):
        inputs.append((left_hbm.at[w, 0], pack_ref.at[pl.ds(w * block, block), :]))
    copies = [
        pltpu.make_async_copy(source, target, sems.at[n])
        for n, (source, target) in enumerate(inputs)
    ]
    for copy in copies:
        copy.start()
    for copy in copies[1:5]:
        copy.wait()
    base = terms * (1 + rights) * block
    lane = lax.broadcasted_iota(jnp.int32, (phys, block), 1)
    row = lax.broadcasted_iota(jnp.int32, (phys, block), 0)
    site = jnp.zeros((phys, block), F32)
    for w in range(terms):
        spot = jnp.where(lane == row + w * phys, 1.0, 0.0).astype(BF16)
        site = site + matmul(site_ref[w], spot)
    pack_ref[base : base + phys, :] = site.astype(BF16)
    numbers = jnp.zeros((SUB, block), F32)
    lane = lax.broadcasted_iota(jnp.int32, (SUB, block), 1)
    for w in range(terms):
        numbers = jnp.where(lane == w, sources_ref[w, own_blk].astype(F32), numbers)
        for b in range(rights):
            at = terms + w * rights + b
            numbers = jnp.where(lane == at, rsource_ref[b, w].astype(F32), numbers)
    for b in range(rights):
        at = terms * (1 + rights) + b
        numbers = jnp.where(lane == at, live_ref[b, own_blk].astype(F32), numbers)
    pack_ref[base + phys : base + phys + SUB, :] = numbers.astype(BF16)
    copies[0].wait()
    for w in range(terms):
        for b in range(rights):
            at = (terms + w * rights + b) * block
            pack_ref[at : at + block, :] = right_ref[w, b].astype(F32).T.astype(BF16)
    for copy in copies[5:]:
        copy.wait()


def block_matrices(terms, rights, numbers, pack, left_ref, right_ref):
    block = pack.shape[-1]
    sectors = left_ref.shape[-1] // block
    for w in range(terms):
        left = pack[w * block : (w + 1) * block, :]
        for r in range(sectors):
            left_ref[w, :, r * block : (r + 1) * block] = jnp.where(
                numbers[0, w] == r, left, jnp.zeros_like(left)
            )
        for b in range(rights):
            start = (terms + w * rights + b) * block
            turned = pack[start : start + block, :]
            source = numbers[0, terms + w * rights + b]
            alive = numbers[0, terms * (1 + rights) + b] != 0
            for r in range(rights):
                right_ref[w, r * block : (r + 1) * block, b * block : (b + 1) * block] = jnp.where(
                    jnp.logical_and(source == r, alive), turned, jnp.zeros_like(turned)
                )


def spread_site(terms, rights, phys, packs, chunks, kron_ref):
    block = packs[0].shape[-1]
    me, own_blk = lax.axis_index("mpo"), lax.axis_index("blk")
    site_at = (1 + rights) * terms * block
    site = jnp.concatenate([p[site_at : site_at + phys, :] for p in packs], axis=1)
    rows, depth = kron_ref.shape
    quarter, here = phys // 4, len(packs) * block
    srow = lax.broadcasted_iota(jnp.int32, (rows, phys), 0) >> 4
    turn = srow >> 2
    owner = lax.bitwise_xor(me, jnp.where(turn == 0, 3, jnp.where(turn == 3, 0, turn)))
    swant = owner * quarter + (srow & 3)
    pick_s = jnp.where(
        lax.broadcasted_iota(jnp.int32, (rows, phys), 1) == swant, 1.0, 0.0
    ).astype(BF16)
    slot = lax.broadcasted_iota(jnp.int32, (1, depth), 1) >> 4
    want = jnp.zeros((1, depth), jnp.int32)
    for n, (shard, pack) in enumerate(chunks):
        state = lax.bitwise_xor(own_blk, shard) * quarter + me
        spot = pack * block + (slot - n * terms) * phys + state
        want = jnp.where(jnp.logical_and(slot >= n * terms, slot < (n + 1) * terms), spot, want)
    pick_t = jnp.where(
        lax.broadcasted_iota(jnp.int32, (here, depth), 0) == want, 1.0, 0.0
    ).astype(BF16)
    spread = matmul(pick_s, matmul(site, pick_t).astype(BF16))
    diagonal = (lax.broadcasted_iota(jnp.int32, (rows, depth), 0) & 15) == (
        lax.broadcasted_iota(jnp.int32, (rows, depth), 1) & 15
    )
    kron_ref[...] = jnp.where(diagonal, spread, 0.0).astype(BF16)


def left_products(left_ref, shards, c_ref, starts, first):
    terms, _, depth = left_ref.shape
    count = c_ref.shape[1]
    left = left_ref[:, first : first + count, :].reshape(terms * count, depth)
    for start, shard in zip(starts, shards):
        c_ref[start : start + terms] = (
            matmul(left, shard[...]).astype(BF16).reshape(terms, count, c_ref.shape[2])
        )


def chosen_products(terms, numbers, pack, shards, c_ref, starts):
    block = pack.shape[-1]
    for w in range(terms):
        row = pl.multiple_of(numbers[0, w] * block, block)
        left = pack[w * block : (w + 1) * block, :]
        for start, shard in zip(starts, shards):
            c_ref[start + w] = matmul(left, shard[pl.ds(row, block), :]).astype(BF16)


def right_products(terms, w_ref, c_ref, y_ref, starts):
    tiles = y_ref.shape[0]
    for w in range(terms):
        for start in starts:
            y = matmul(c_ref[start + w], w_ref[w]).astype(BF16)
            at = (start + w) * SUB
            y_ref[:, at : at + SUB, :] = y.reshape(tiles, SUB, y.shape[-1])


class Plan:
    def __init__(self, packs, chunks, made=(), before=True, prepare_last=False, last=None):
        self.packs, self.chunks, self.made = packs, chunks, made
        self.before, self.prepare_last, self.last = before, prepare_last, last
        self.used = sorted({k for _, k in chunks})
        self.given = [k for k in self.used if k not in made]
        self.shards = sorted({q for q, _ in chunks})


def terms_body(terms, rights, phys, plan, *refs):
    refs = list(refs)

    def take(count):
        taken, refs[:] = refs[:count], refs[count:]
        return taken

    last = plan.last is not None
    numbers = dict(zip(plan.made, take(len(plan.made))))
    packs = take(0 if last else plan.packs)
    lefts = dict(zip(plan.given, take(len(plan.given))))
    rights_of = dict(zip(plan.given, take(len(plan.given))))
    shards = dict(zip(plan.shards, take(len(plan.shards))))
    acc_in = take(1)[0] if plan.before else None
    kron_ref = take(1)[0] if last else None
    lefts.update(zip(plan.made, take(len(plan.made))))
    rights_of.update(zip(plan.made, take(len(plan.made))))
    if plan.prepare_last:
        spread_site(terms, rights, phys, packs, [(3, k) for k in range(plan.packs)], take(1)[0])
    targets = take(3 if last else 1)
    c_ref, y_ref = take(2)
    if not last:
        kron_ref = take(1)[0]
        spread_site(terms, rights, phys, packs, plan.chunks, kron_ref)
    for k in plan.made:
        block_matrices(terms, rights, numbers[k], packs[k], lefts[k], rights_of[k])
    starts = {k: [n * terms for n, (_, pack) in enumerate(plan.chunks) if pack == k] for k in plan.used}
    first = plan.last * c_ref.shape[1] if last else 0
    for k in plan.used:
        sources = [shards[q] for q, pack in plan.chunks if pack == k]
        if k in plan.made:
            chosen_products(terms, numbers[k], packs[k], sources, c_ref, starts[k])
        else:
            left_products(lefts[k], sources, c_ref, starts[k], first)
    for k in plan.used:
        right_products(terms, rights_of[k], c_ref, y_ref, starts[k])
    for i in range(y_ref.shape[0]):
        total = matmul(kron_ref[...], y_ref[i])
        if plan.before:
            total = total + acc_in[first // SUB + i]
        if not last:
            targets[0][i] = total
            continue
        width = total.shape[1]
        count = total.shape[0] // SUB // 4
        for n, (target, place) in enumerate(
            ((targets[0], 0), (targets[0], 1), (targets[1], 0), (targets[2], 0))
        ):
            for m in range(count):
                start, column = (n * count + m) * SUB, (place * count + m) * width
                target[i * SUB : (i + 1) * SUB, column : column + width] = total[
                    start : start + SUB, :
                ].astype(target.dtype)


def in_hbm(x):
    return pltpu.with_memory_space_constraint(x, pltpu.HBM)


def call(body, out_shape, in_specs, scratch=(), out_specs=None, name=None, vmem=VMEM_BYTES, flops=1000):
    extra = {} if out_specs is None else {"out_specs": out_specs}
    return pl.pallas_call(
        body,
        out_shape=out_shape,
        in_specs=in_specs,
        scratch_shapes=scratch,
        compiler_params=pltpu.CompilerParams(vmem_limit_bytes=vmem),
        cost_estimate=pl.CostEstimate(flops=flops, bytes_accessed=1000, transcendentals=0),
        name=name,
        **extra,
    )


def by_states(
    wavefunction, left_blocks, right_blocks, site_terms, left_source, right_source, live_pairs
):
    all_rows = wavefunction.shape[0]
    terms, _, block, _ = left_blocks.shape
    rights = right_blocks.shape[1]
    phys = site_terms.shape[1]
    width = rights * block
    slots = 4
    rows = phys * SUB
    tiles = block // SUB
    smem = pl.BlockSpec(memory_space=pltpu.SMEM)
    vmem = pl.BlockSpec(memory_space=pltpu.VMEM)
    hbm = pl.BlockSpec(memory_space=pltpu.HBM)

    pack_rows = terms * (1 + rights) * block + phys + SUB
    mine = call(
        slice_body,
        jax.ShapeDtypeStruct((all_rows, width), BF16),
        [hbm],
        [pltpu.SemaphoreType.DMA],
        out_specs=vmem,
        name="own_states",
        vmem=SLICE_BYTES,
    )(in_hbm(wavefunction))

    def swap(x):
        return lax.ppermute(x, "mpo", CORE)

    pack = call(
        functools.partial(pack_body, terms, rights, phys),
        jax.ShapeDtypeStruct((pack_rows, block), BF16),
        [hbm] * 6,
        [
            pltpu.VMEM(right_blocks.shape, BF16),
            pltpu.VMEM(site_terms.shape, BF16),
            pltpu.SMEM(left_source.shape, jnp.int32),
            pltpu.SMEM(right_source.T.shape, jnp.int32),
            pltpu.SMEM(live_pairs.T.shape, jnp.int32),
            pltpu.SemaphoreType.DMA((terms + 5,)),
        ],
        out_specs=vmem,
        name="pack_operators",
        vmem=PACK_BYTES,
    )(
        *[
            in_hbm(x)
            for x in (
                left_blocks, right_blocks, site_terms, left_source, right_source.T, live_pairs.T
            )
        ]
    )

    def numbers_of(p):
        return p[pack_rows - SUB : pack_rows - SUB + 1, :].astype(jnp.int32)

    one_pack = terms * SUB

    def run(name, plan, packs, numbers, shards, acc=None, given=(), kron=None, flops=1000):
        depth = len(plan.chunks) * one_pack
        last = plan.last is not None
        part = PARTS if last else 1
        shapes = [jax.ShapeDtypeStruct((terms, block, all_rows), BF16) for _ in plan.made]
        shapes += [jax.ShapeDtypeStruct((terms, width, width), BF16) for _ in plan.made]
        if plan.prepare_last:
            shapes.append(jax.ShapeDtypeStruct((rows, len(packs) * one_pack), BF16))
        if last:
            size, columns = block // part, phys // slots * width
            shapes.append(jax.ShapeDtypeStruct((size, 2 * columns), BF16))
            shapes += [jax.ShapeDtypeStruct((size, columns), F32)] * 2
        else:
            shapes.append(jax.ShapeDtypeStruct((tiles, rows, width), F32))
        lefts, rights_of = [g[0] for g in given], [g[1] for g in given]
        arrays = [*packs, *lefts, *rights_of, *shards]
        arrays += [a for a in (acc, kron) if a is not None]
        scratch = [
            pltpu.VMEM((len(plan.chunks) * terms, block // part, width), BF16),
            pltpu.VMEM((tiles // part, depth, width), BF16),
        ]
        if not last:
            scratch.append(pltpu.VMEM((rows, depth), BF16))
        outs = call(
            functools.partial(terms_body, terms, rights, phys, plan),
            tuple(shapes),
            [smem] * len(numbers) + [vmem] * len(arrays),
            scratch,
            name=name,
            flops=flops,
        )(*numbers, *arrays)
        made = len(plan.made)
        return tuple(zip(outs[:made], outs[made : 2 * made])) + tuple(outs[2 * made :])

    far = lax.ppermute(mine, "blk", FAR)
    near = lax.ppermute(mine, "blk", NEAR)
    pack_x = lax.ppermute(pack, "mpo", ACROSS)
    own, acc = run(
        "own_pack_own_shard",
        Plan(1, [(0, 0)], made=(0,), before=False),
        (pack,),
        (numbers_of(pack),),
        (mine,),
        flops=OWN_FLOPS,
    )
    pack_c = swap(pack)
    far, acc, mine = lax.optimization_barrier((far, acc, mine))
    farthest = lax.ppermute(far, "blk", NEAR)
    (acc,) = run(
        "own_pack_near_far",
        Plan(1, [(1, 0), (2, 0)]),
        (pack,),
        (),
        (near, far),
        acc,
        (own,),
        flops=CHIP_FLOPS,
    )
    acc, pack_x, pack_c = lax.optimization_barrier((acc, pack_x, pack_c))
    x_packs = (pack_x, swap(pack_x))
    core, acc = run(
        "core_pack",
        Plan(1, [(0, 0), (1, 0), (2, 0)], made=(0,)),
        (pack_c,),
        (numbers_of(pack_c),),
        (mine, near, far),
        acc,
        flops=CORE_FLOPS,
    )
    across, beyond, kron, acc = run(
        "other_packs",
        Plan(4, [(q, k) for q in (0, 1, 2) for k in (2, 3)], made=(2, 3), prepare_last=True),
        (pack, pack_c, *x_packs),
        [numbers_of(p) for p in x_packs],
        (mine, near, far),
        acc,
    )
    farthest, acc = lax.optimization_barrier((farthest, acc))
    outs = []
    for part in range(PARTS):
        give, keep_x, keep = run(
            "third_shard",
            Plan(4, [(3, k) for k in range(4)], last=part),
            (),
            (),
            (farthest,),
            acc,
            (own, core, across, beyond),
            kron,
        )
        columns = keep.shape[1]
        back = swap(give)
        send = (keep_x + back[:, :columns].astype(F32)).astype(BF16)
        taken = lax.ppermute(send, "mpo", ACROSS)
        outs.append((keep + back[:, columns:].astype(F32) + taken.astype(F32)).astype(BF16))
    return jnp.concatenate(outs, axis=0) if PARTS > 1 else outs[0]


def solution(mesh):
    sizes = dict(mesh.shape)

    def on_device(
        wavefunction, left_blocks, right_blocks, site_terms, left_source, right_source, live_pairs
    ):
        columns = wavefunction.shape[1]
        terms, sectors, block, _ = left_blocks.shape
        phys, rights = site_terms.shape[1], right_blocks.shape[1]
        square = sizes["blk"] == 4 and sizes["mpo"] == 4 and sectors == 1 and rights == 2
        fits = columns == 4 * rights * block and phys == 16 and block == 128 and terms == 4
        step = by_states if square and fits else by_terms
        return step(
            wavefunction, left_blocks, right_blocks, site_terms, left_source, right_source, live_pairs
        )

    return jax.shard_map(
        on_device,
        mesh=mesh,
        in_specs=(
            P("rep", "blk"),
            P(("rep", "mpo"), "blk", None, None),
            P(("rep", "mpo"), None, None, None),
            P(("rep", "mpo"), None, None),
            P(("rep", "mpo"), None),
            P(("rep", "mpo"), None),
            P("rep", None),
        ),
        out_specs=P(("rep", "blk"), "mpo"),
        check_vma=False,
    )
```

```python
import functools

import jax
import jax.numpy as jnp
from jax import lax
from jax.experimental import pallas as pl
from jax.experimental.pallas import tpu as pltpu
from jax.sharding import PartitionSpec as P

F32 = jnp.float32
BF16 = jnp.bfloat16
VMEM_BYTES = 32 * 1024 * 1024
SLICE_BYTES = 32 * 1024 * 1024
PACK_BYTES = 32 * 1024 * 1024
OWN_FLOPS = 1000
CHIP_FLOPS = int(8e9)
CORE_FLOPS = int(3e9)
NEAR = ((0, 1), (1, 0), (2, 3), (3, 2))
FAR = ((0, 2), (2, 0), (1, 3), (3, 1))
CORE = ((0, 1), (1, 0), (2, 3), (3, 2))
ACROSS = ((0, 2), (2, 0), (1, 3), (3, 1))
PARTS = 2
SUB = 16


def carry_left(blocks, sources, pieces):
    picked = jnp.take(blocks, sources, axis=0)
    return jnp.einsum(
        "...aij,...ajc->...aic", pieces, picked, preferred_element_type=F32
    ).astype(BF16)


def apply_right(received, site_one, source_one, right_one, physical, right_count, block_rows):
    shaped = received.reshape(received.shape[0], physical, right_count, block_rows)
    turned = jnp.einsum(
        "st,itrj->isrj", site_one, shaped, preferred_element_type=F32
    ).astype(BF16)
    picked = jnp.take(turned, source_one, axis=2)
    return jnp.einsum("isbj,bkj->isbk", picked, right_one, preferred_element_type=F32)


def by_terms(
    wavefunction, left_blocks, right_blocks, site_terms, left_source, right_source, live_pairs
):
    all_rows, columns = wavefunction.shape
    term_count, own_sectors, block_rows = left_blocks.shape[:3]
    physical = site_terms.shape[1]
    right_count = right_blocks.shape[1]
    own_rows = own_sectors * block_rows
    blocks = wavefunction.reshape(all_rows // block_rows, block_rows, columns)
    accumulated = jnp.zeros((own_rows, physical, right_count, block_rows), F32)
    for member in range(term_count):
        pieces = lax.all_gather(left_blocks[member], "blk", axis=0, tiled=True)
        carried = carry_left(blocks, left_source[member], pieces)
        received = lax.all_to_all(
            carried.reshape(all_rows, columns), "blk", split_axis=0, concat_axis=1, tiled=True
        )
        accumulated = accumulated + apply_right(
            received,
            site_terms[member],
            right_source[member],
            right_blocks[member],
            physical,
            right_count,
            block_rows,
        )
    position = lax.axis_index("blk")
    live_rows = lax.dynamic_slice_in_dim(live_pairs, position * own_sectors, own_sectors, 0)
    row_mask = jnp.repeat(live_rows.astype(F32), block_rows, axis=0)
    accumulated = accumulated * row_mask[:, None, :, None]
    flattened = accumulated.reshape(own_rows, physical * right_count * block_rows)
    summed = lax.psum_scatter(flattened, "mpo", scatter_dimension=1, tiled=True)
    return summed.astype(BF16)


def matmul(a, b):
    return jnp.dot(a, b, preferred_element_type=F32)


def slice_body(wave_ref, own_ref, sem):
    width = own_ref.shape[1]
    start = pl.multiple_of(lax.axis_index("mpo") * width, width)
    copy = pltpu.make_async_copy(wave_ref.at[:, pl.ds(start, width)], own_ref, sem)
    copy.start()
    copy.wait()


def pack_body(
    terms, rights, phys, left_hbm, right_hbm, site_hbm, sources_hbm, rsource_hbm, live_hbm,
    pack_ref, right_ref, site_ref, sources_ref, rsource_ref, live_ref, sems,
):
    block = right_ref.shape[-1]
    own_blk = lax.axis_index("blk")
    inputs = [
        (right_hbm, right_ref),
        (site_hbm, site_ref),
        (sources_hbm, sources_ref),
        (rsource_hbm, rsource_ref),
        (live_hbm, live_ref),
    ]
    for w in range(terms):
        inputs.append((left_hbm.at[w, 0], pack_ref.at[pl.ds(w * block, block), :]))
    copies = [
        pltpu.make_async_copy(source, target, sems.at[n])
        for n, (source, target) in enumerate(inputs)
    ]
    for copy in copies:
        copy.start()
    for copy in copies[1:5]:
        copy.wait()
    base = terms * (1 + rights) * block
    lane = lax.broadcasted_iota(jnp.int32, (phys, block), 1)
    row = lax.broadcasted_iota(jnp.int32, (phys, block), 0)
    site = jnp.zeros((phys, block), F32)
    for w in range(terms):
        spot = jnp.where(lane == row + w * phys, 1.0, 0.0).astype(BF16)
        site = site + matmul(site_ref[w], spot)
    pack_ref[base : base + phys, :] = site.astype(BF16)
    numbers = jnp.zeros((SUB, block), F32)
    lane = lax.broadcasted_iota(jnp.int32, (SUB, block), 1)
    for w in range(terms):
        numbers = jnp.where(lane == w, sources_ref[w, own_blk].astype(F32), numbers)
        for b in range(rights):
            at = terms + w * rights + b
            numbers = jnp.where(lane == at, rsource_ref[b, w].astype(F32), numbers)
    for b in range(rights):
        at = terms * (1 + rights) + b
        numbers = jnp.where(lane == at, live_ref[b, own_blk].astype(F32), numbers)
    pack_ref[base + phys : base + phys + SUB, :] = numbers.astype(BF16)
    copies[0].wait()
    for w in range(terms):
        for b in range(rights):
            at = (terms + w * rights + b) * block
            pack_ref[at : at + block, :] = right_ref[w, b].astype(F32).T.astype(BF16)
    for copy in copies[5:]:
        copy.wait()


def block_matrices(terms, rights, numbers, pack, left_ref, right_ref):
    block = pack.shape[-1]
    sectors = left_ref.shape[-1] // block
    for w in range(terms):
        left = pack[w * block : (w + 1) * block, :]
        for r in range(sectors):
            left_ref[w, :, r * block : (r + 1) * block] = jnp.where(
                numbers[0, w] == r, left, jnp.zeros_like(left)
            )
        for b in range(rights):
            start = (terms + w * rights + b) * block
            turned = pack[start : start + block, :]
            source = numbers[0, terms + w * rights + b]
            alive = numbers[0, terms * (1 + rights) + b] != 0
            for r in range(rights):
                right_ref[w, r * block : (r + 1) * block, b * block : (b + 1) * block] = jnp.where(
                    jnp.logical_and(source == r, alive), turned, jnp.zeros_like(turned)
                )


def spread_site(terms, rights, phys, packs, chunks, kron_ref):
    block = packs[0].shape[-1]
    me, own_blk = lax.axis_index("mpo"), lax.axis_index("blk")
    site_at = (1 + rights) * terms * block
    site = jnp.concatenate([p[site_at : site_at + phys, :] for p in packs], axis=1)
    rows, depth = kron_ref.shape
    quarter, here = phys // 4, len(packs) * block
    srow = lax.broadcasted_iota(jnp.int32, (rows, phys), 0) >> 4
    turn = srow >> 2
    owner = lax.bitwise_xor(me, jnp.where(turn == 0, 3, jnp.where(turn == 3, 0, turn)))
    swant = owner * quarter + (srow & 3)
    pick_s = jnp.where(
        lax.broadcasted_iota(jnp.int32, (rows, phys), 1) == swant, 1.0, 0.0
    ).astype(BF16)
    slot = lax.broadcasted_iota(jnp.int32, (1, depth), 1) >> 4
    want = jnp.zeros((1, depth), jnp.int32)
    for n, (shard, pack) in enumerate(chunks):
        state = lax.bitwise_xor(own_blk, shard) * quarter + me
        spot = pack * block + (slot - n * terms) * phys + state
        want = jnp.where(jnp.logical_and(slot >= n * terms, slot < (n + 1) * terms), spot, want)
    pick_t = jnp.where(
        lax.broadcasted_iota(jnp.int32, (here, depth), 0) == want, 1.0, 0.0
    ).astype(BF16)
    spread = matmul(pick_s, matmul(site, pick_t).astype(BF16))
    diagonal = (lax.broadcasted_iota(jnp.int32, (rows, depth), 0) & 15) == (
        lax.broadcasted_iota(jnp.int32, (rows, depth), 1) & 15
    )
    kron_ref[...] = jnp.where(diagonal, spread, 0.0).astype(BF16)


def left_products(left_ref, shards, c_ref, starts, first):
    terms, _, depth = left_ref.shape
    count = c_ref.shape[1]
    left = left_ref[:, first : first + count, :].reshape(terms * count, depth)
    for start, shard in zip(starts, shards):
        c_ref[start : start + terms] = (
            matmul(left, shard[...]).astype(BF16).reshape(terms, count, c_ref.shape[2])
        )


def chosen_products(terms, numbers, pack, shards, c_ref, starts):
    block = pack.shape[-1]
    for w in range(terms):
        row = pl.multiple_of(numbers[0, w] * block, block)
        left = pack[w * block : (w + 1) * block, :]
        for start, shard in zip(starts, shards):
            c_ref[start + w] = matmul(left, shard[pl.ds(row, block), :]).astype(BF16)


def right_products(terms, w_ref, c_ref, y_ref, starts):
    tiles = y_ref.shape[0]
    for w in range(terms):
        for start in starts:
            y = matmul(c_ref[start + w], w_ref[w]).astype(BF16)
            at = (start + w) * SUB
            y_ref[:, at : at + SUB, :] = y.reshape(tiles, SUB, y.shape[-1])


class Plan:
    def __init__(self, packs, chunks, made=(), before=True, prepare_last=False, last=None):
        self.packs, self.chunks, self.made = packs, chunks, made
        self.before, self.prepare_last, self.last = before, prepare_last, last
        self.used = sorted({k for _, k in chunks})
        self.given = [k for k in self.used if k not in made]
        self.shards = sorted({q for q, _ in chunks})


def terms_body(terms, rights, phys, plan, *refs):
    refs = list(refs)

    def take(count):
        taken, refs[:] = refs[:count], refs[count:]
        return taken

    last = plan.last is not None
    numbers = dict(zip(plan.made, take(len(plan.made))))
    packs = take(0 if last else plan.packs)
    lefts = dict(zip(plan.given, take(len(plan.given))))
    rights_of = dict(zip(plan.given, take(len(plan.given))))
    shards = dict(zip(plan.shards, take(len(plan.shards))))
    acc_in = take(1)[0] if plan.before else None
    kron_ref = take(1)[0] if last else None
    lefts.update(zip(plan.made, take(len(plan.made))))
    rights_of.update(zip(plan.made, take(len(plan.made))))
    if plan.prepare_last:
        spread_site(terms, rights, phys, packs, [(3, k) for k in range(plan.packs)], take(1)[0])
    targets = take(3 if last else 1)
    c_ref, y_ref = take(2)
    if not last:
        kron_ref = take(1)[0]
        spread_site(terms, rights, phys, packs, plan.chunks, kron_ref)
    for k in plan.made:
        block_matrices(terms, rights, numbers[k], packs[k], lefts[k], rights_of[k])
    starts = {k: [n * terms for n, (_, pack) in enumerate(plan.chunks) if pack == k] for k in plan.used}
    first = plan.last * c_ref.shape[1] if last else 0
    for k in plan.used:
        sources = [shards[q] for q, pack in plan.chunks if pack == k]
        if k in plan.made:
            chosen_products(terms, numbers[k], packs[k], sources, c_ref, starts[k])
        else:
            left_products(lefts[k], sources, c_ref, starts[k], first)
    for k in plan.used:
        right_products(terms, rights_of[k], c_ref, y_ref, starts[k])
    for i in range(y_ref.shape[0]):
        total = matmul(kron_ref[...], y_ref[i])
        if plan.before:
            total = total + acc_in[first // SUB + i]
        if not last:
            targets[0][i] = total
            continue
        width = total.shape[1]
        count = total.shape[0] // SUB // 4
        for n, (target, place) in enumerate(
            ((targets[0], 0), (targets[0], 1), (targets[1], 0), (targets[2], 0))
        ):
            for m in range(count):
                start, column = (n * count + m) * SUB, (place * count + m) * width
                target[i * SUB : (i + 1) * SUB, column : column + width] = total[
                    start : start + SUB, :
                ].astype(target.dtype)


def third_body(terms, packs, *refs):
    lefts, rights_of, (shard, acc_in, kron_ref) = refs[:packs], refs[packs : 2 * packs], refs[2 * packs : 2 * packs + 3]
    (*gives, y_ref), c_ref = refs[2 * packs + 3 : -1], refs[-1]
    for k in range(packs):
        left_products(lefts[k], [shard], c_ref, [k * terms], 0)
    for k in range(packs):
        right_products(terms, rights_of[k], c_ref, y_ref, [k * terms])
    quarter = kron_ref.shape[0] // 4
    tiles = y_ref.shape[0]
    for i in range(tiles):
        total = matmul(kron_ref[0:quarter, :], y_ref[i]) + acc_in[i, 0:quarter, :]
        put_tile(gives, i, tiles, total)


def put_tile(targets, tile, tiles, total):
    each = tiles // len(targets)
    target, first = targets[tile // each], tile % each * SUB
    width = total.shape[1]
    for m in range(total.shape[0] // SUB):
        target[first : first + SUB, m * width : (m + 1) * width] = total[
            m * SUB : (m + 1) * SUB, :
        ].astype(target.dtype)


def sums_body(y_ref, acc_in, kron_ref, core_ref, *refs):
    keeps_x, keep_ref = refs[:-1], refs[-1]
    quarter = kron_ref.shape[0] // 4
    tiles = y_ref.shape[0]
    for i in range(tiles):
        total = matmul(kron_ref[quarter:, :], y_ref[i]) + acc_in[i, quarter:, :]
        for n, targets in enumerate(((core_ref,), keeps_x, (keep_ref,))):
            put_tile(targets, i, tiles, total[n * quarter : (n + 1) * quarter, :])


def in_hbm(x):
    return pltpu.with_memory_space_constraint(x, pltpu.HBM)


def call(body, out_shape, in_specs, scratch=(), out_specs=None, name=None, vmem=VMEM_BYTES, flops=1000):
    extra = {} if out_specs is None else {"out_specs": out_specs}
    return pl.pallas_call(
        body,
        out_shape=out_shape,
        in_specs=in_specs,
        scratch_shapes=scratch,
        compiler_params=pltpu.CompilerParams(vmem_limit_bytes=vmem),
        cost_estimate=pl.CostEstimate(flops=flops, bytes_accessed=1000, transcendentals=0),
        name=name,
        **extra,
    )


def by_states(
    wavefunction, left_blocks, right_blocks, site_terms, left_source, right_source, live_pairs
):
    all_rows = wavefunction.shape[0]
    terms, _, block, _ = left_blocks.shape
    rights = right_blocks.shape[1]
    phys = site_terms.shape[1]
    width = rights * block
    slots = 4
    rows = phys * SUB
    tiles = block // SUB
    smem = pl.BlockSpec(memory_space=pltpu.SMEM)
    vmem = pl.BlockSpec(memory_space=pltpu.VMEM)
    hbm = pl.BlockSpec(memory_space=pltpu.HBM)

    pack_rows = terms * (1 + rights) * block + phys + SUB
    mine = call(
        slice_body,
        jax.ShapeDtypeStruct((all_rows, width), BF16),
        [hbm],
        [pltpu.SemaphoreType.DMA],
        out_specs=vmem,
        name="own_states",
        vmem=SLICE_BYTES,
    )(in_hbm(wavefunction))

    def swap(x):
        return lax.ppermute(x, "mpo", CORE)

    pack = call(
        functools.partial(pack_body, terms, rights, phys),
        jax.ShapeDtypeStruct((pack_rows, block), BF16),
        [hbm] * 6,
        [
            pltpu.VMEM(right_blocks.shape, BF16),
            pltpu.VMEM(site_terms.shape, BF16),
            pltpu.SMEM(left_source.shape, jnp.int32),
            pltpu.SMEM(right_source.T.shape, jnp.int32),
            pltpu.SMEM(live_pairs.T.shape, jnp.int32),
            pltpu.SemaphoreType.DMA((terms + 5,)),
        ],
        out_specs=vmem,
        name="pack_operators",
        vmem=PACK_BYTES,
    )(
        *[
            in_hbm(x)
            for x in (
                left_blocks, right_blocks, site_terms, left_source, right_source.T, live_pairs.T
            )
        ]
    )

    def numbers_of(p):
        return p[pack_rows - SUB : pack_rows - SUB + 1, :].astype(jnp.int32)

    one_pack = terms * SUB

    def run(name, plan, packs, numbers, shards, acc=None, given=(), kron=None, flops=1000):
        depth = len(plan.chunks) * one_pack
        last = plan.last is not None
        part = PARTS if last else 1
        shapes = [jax.ShapeDtypeStruct((terms, block, all_rows), BF16) for _ in plan.made]
        shapes += [jax.ShapeDtypeStruct((terms, width, width), BF16) for _ in plan.made]
        if plan.prepare_last:
            shapes.append(jax.ShapeDtypeStruct((rows, len(packs) * one_pack), BF16))
        if last:
            size, columns = block // part, phys // slots * width
            shapes.append(jax.ShapeDtypeStruct((size, 2 * columns), BF16))
            shapes += [jax.ShapeDtypeStruct((size, columns), F32)] * 2
        else:
            shapes.append(jax.ShapeDtypeStruct((tiles, rows, width), F32))
        lefts, rights_of = [g[0] for g in given], [g[1] for g in given]
        arrays = [*packs, *lefts, *rights_of, *shards]
        arrays += [a for a in (acc, kron) if a is not None]
        scratch = [
            pltpu.VMEM((len(plan.chunks) * terms, block // part, width), BF16),
            pltpu.VMEM((tiles // part, depth, width), BF16),
        ]
        if not last:
            scratch.append(pltpu.VMEM((rows, depth), BF16))
        outs = call(
            functools.partial(terms_body, terms, rights, phys, plan),
            tuple(shapes),
            [smem] * len(numbers) + [vmem] * len(arrays),
            scratch,
            name=name,
            flops=flops,
        )(*numbers, *arrays)
        made = len(plan.made)
        return tuple(zip(outs[:made], outs[made : 2 * made])) + tuple(outs[2 * made :])

    far = lax.ppermute(mine, "blk", FAR)
    near = lax.ppermute(mine, "blk", NEAR)
    pack_x = lax.ppermute(pack, "mpo", ACROSS)
    own, acc = run(
        "own_pack_own_shard",
        Plan(1, [(0, 0)], made=(0,), before=False),
        (pack,),
        (numbers_of(pack),),
        (mine,),
        flops=OWN_FLOPS,
    )
    pack_c = swap(pack)
    far, acc, mine = lax.optimization_barrier((far, acc, mine))
    farthest = lax.ppermute(far, "blk", NEAR)
    (acc,) = run(
        "own_pack_near_far",
        Plan(1, [(1, 0), (2, 0)]),
        (pack,),
        (),
        (near, far),
        acc,
        (own,),
        flops=CHIP_FLOPS,
    )
    acc, pack_x, pack_c = lax.optimization_barrier((acc, pack_x, pack_c))
    x_packs = (pack_x, swap(pack_x))
    core, acc = run(
        "core_pack",
        Plan(1, [(0, 0), (1, 0), (2, 0)], made=(0,)),
        (pack_c,),
        (numbers_of(pack_c),),
        (mine, near, far),
        acc,
        flops=CORE_FLOPS,
    )
    across, beyond, kron, acc = run(
        "other_packs",
        Plan(4, [(q, k) for q in (0, 1, 2) for k in (2, 3)], made=(2, 3), prepare_last=True),
        (pack, pack_c, *x_packs),
        [numbers_of(p) for p in x_packs],
        (mine, near, far),
        acc,
    )
    farthest, acc = lax.optimization_barrier((farthest, acc))
    given = (own, core, across, beyond)
    columns = phys // slots * width
    part_shape = (block // PARTS, columns)
    *gives, y = call(
        functools.partial(third_body, terms, len(given)),
        (
            *[jax.ShapeDtypeStruct(part_shape, BF16)] * PARTS,
            jax.ShapeDtypeStruct((tiles, len(given) * one_pack, width), BF16),
        ),
        [vmem] * (2 * len(given) + 3),
        [pltpu.VMEM((len(given) * terms, block, width), BF16)],
        name="third_shard",
    )(*[g[0] for g in given], *[g[1] for g in given], farthest, acc, kron)
    core_sum, *keeps_x, keep = call(
        sums_body,
        (
            jax.ShapeDtypeStruct((block, columns), BF16),
            *[jax.ShapeDtypeStruct(part_shape, F32)] * PARTS,
            jax.ShapeDtypeStruct((block, columns), F32),
        ),
        [vmem] * 3,
        name="sums",
    )(y, acc, kron)
    taken = []
    for give, keep_x in zip(gives, keeps_x):
        send = (keep_x + swap(give).astype(F32)).astype(BF16)
        taken.append(lax.ppermute(send, "mpo", ACROSS))
    kept = keep + swap(core_sum).astype(F32)
    size = block // PARTS
    outs = [
        (kept[n * size : (n + 1) * size] + part.astype(F32)).astype(BF16)
        for n, part in enumerate(taken)
    ]
    return jnp.concatenate(outs, axis=0)


def solution(mesh):
    sizes = dict(mesh.shape)

    def on_device(
        wavefunction, left_blocks, right_blocks, site_terms, left_source, right_source, live_pairs
    ):
        columns = wavefunction.shape[1]
        terms, sectors, block, _ = left_blocks.shape
        phys, rights = site_terms.shape[1], right_blocks.shape[1]
        square = sizes["blk"] == 4 and sizes["mpo"] == 4 and sectors == 1 and rights == 2
        fits = columns == 4 * rights * block and phys == 16 and block == 128 and terms == 4
        step = by_states if square and fits else by_terms
        return step(
            wavefunction, left_blocks, right_blocks, site_terms, left_source, right_source, live_pairs
        )

    return jax.shard_map(
        on_device,
        mesh=mesh,
        in_specs=(
            P("rep", "blk"),
            P(("rep", "mpo"), "blk", None, None),
            P(("rep", "mpo"), None, None, None),
            P(("rep", "mpo"), None, None),
            P(("rep", "mpo"), None),
            P(("rep", "mpo"), None),
            P("rep", None),
        ),
        out_specs=P(("rep", "blk"), "mpo"),
        check_vma=False,
    )
```
